512 devices in a mesh: layer: 8 (over z_lo), row: 8 (over x, core), col: 8 (over z_hi, y).
Axes of the slice: x: 4, y: 4, z: 16 (z_hi: 2, z_lo: 8; z = z_hi * 8 + z_lo), core: 2. Of those that a mesh axis runs over, the one named last changes fastest.
Arguments:
- grad: bfloat16 [40960, 1024], P(('layer', 'row'), 'col'), parts along dimension 0, may hold values from -6 to 6
- left_basis: bfloat16 [40960, 5120], P(('layer', 'row'), 'col'), parts along dimension 0, may hold values from -0.078125 to 0.078125
- right_rows: bfloat16 [8192, 1024], P('layer', 'col'), parts along dimension 0, may hold values from -0.1875 to 0.1875
- exp_avg: float32 [40960, 1024], P(('layer', 'col'), 'row'), parts along dimension 0, may hold values from -2 to 2
- exp_avg_sq: float32 [40960, 1024], P(('layer', 'col'), 'row'), parts along dimension 0, may hold values from 0.05 to 2
Outputs:
- update: bfloat16 [40960, 1024], P(('layer', 'row'), 'col'), parts along dimension 0
- exp_avg_new: float32 [40960, 1024], P(('layer', 'col'), 'row'), parts along dimension 0
- exp_avg_sq_new: float32 [40960, 1024], P(('layer', 'col'), 'row'), parts along dimension 0
- left_gram: float32 [40960, 5120], P(('layer', 'row'), 'col'), parts along dimension 0
- right_gram: float32 [8192, 1024], P(('layer', 'col'), 'row'), parts along dimension 0
The draws below stay inside these ranges and needn't reach their ends.
There are 8 independent parts, one for each index of `layer`. The reference program is written for one: setup_inputs(seed, part) draws one part's arguments, and reference() takes and returns one part's arrays. A program takes and returns all parts, laid end to end along the dimension named above; each array names one. Nothing has to cross between parts.
All inputs are finite; a program needn't handle non-finite values.
Results may differ from the reference program's by a relative error of at most 0.02.
Values may be sent and summed in bfloat16 or wider, within the bound.
No kernel may reach another device: no remote copies, remote signals or barrier semaphores. Data moves between devices by JAX's collectives and lax.ppermute only.
A program may use at most 64 MiB of HBM per device.

```python
import math
import jax
import jax.numpy as jnp
from jax import lax

M = 5120
C = 1024
N_ROW = 8
N_COL = 8


def block_scale(stream_key, dims, pieces, low, top_value):
    def one(dim, shards_of):
        draws = jax.random.uniform(jax.random.fold_in(jax.random.fold_in(stream_key, 6), dim), (shards_of,), jnp.float32, low / len(pieces), top_value / len(pieces))
        return jnp.repeat(jnp.exp(draws), dims[dim] // shards_of).reshape((-1,) + (1,) * (len(dims) - dim - 1))

    gain = one(*pieces[0])
    for cut in pieces[1:]:
        gain = gain * one(*cut)
    return gain


def gaussian(key, dims, spread, most, cuts=(), dtype=jnp.bfloat16):
    drawn = spread * jax.random.normal(key, dims, jnp.float32)
    if cuts:
        drawn = drawn * block_scale(key, dims, cuts, -0.22, 0.18)
    return jnp.clip(drawn, -most, most).astype(dtype)


def setup_inputs(seed: int = 0, part: int = 0) -> dict:
    keys = jax.random.split(jax.random.key(seed), 6)
    part_keys = jax.random.split(jax.random.fold_in(keys[5], part), 6)
    return {
        "grad": gaussian(part_keys[0], (M, C), 1.0, 6.0, ((0, 8), (1, 8))),
        "left_basis": gaussian(part_keys[1], (M, M), M ** -0.5, 0.078125, ((0, 8), (1, 8))),
        "right_rows": gaussian(part_keys[2], (C, C), C ** -0.5, 0.1875, ((1, 8),)),
        "exp_avg": gaussian(part_keys[3], (M, C), 0.3, 2.0, ((0, 8), (1, 8)), jnp.float32),
        "exp_avg_sq": jnp.clip(jnp.exp(math.log(2.0) - 3.6888794 * jax.random.uniform(part_keys[4], (M, C), jnp.float32) ** block_scale(part_keys[4], (M, C), ((0, 8), (1, 8)), -0.2, 0.2)), 0.05, 2.0),
    }


first_beta = 0.9
second_beta = 0.95
epsilon = 1e-08

def rounded(value):
    return lax.optimization_barrier(value.astype(jnp.bfloat16)).astype(jnp.float32)

def reference(grad, left_basis, right_rows, exp_avg, exp_avg_sq):
    rotated_right = jnp.dot(grad, right_rows.T, preferred_element_type=jnp.float32).astype(jnp.bfloat16)
    row_block = M // N_ROW
    rotated = jnp.zeros((M, C), jnp.float32)
    right_gram = jnp.zeros((C, C), jnp.float32)
    for block in range(N_ROW):
        lower = block * row_block
        basis_rows = left_basis[lower:lower + row_block, :]
        right_part = rotated_right[lower:lower + row_block, :]
        grad_part = grad[lower:lower + row_block, :]
        rotated = rotated + rounded(jnp.dot(basis_rows.T, right_part, preferred_element_type=jnp.float32))
        right_gram = right_gram + rounded(jnp.dot(grad_part.T, grad_part, preferred_element_type=jnp.float32) * (1.0 / M))
    exp_avg_new = first_beta * exp_avg + (1.0 - first_beta) * rotated
    exp_avg_sq_new = second_beta * exp_avg_sq + (1.0 - second_beta) * rotated * rotated
    direction = (exp_avg_new / (jnp.sqrt(exp_avg_sq_new) + epsilon)).astype(jnp.bfloat16)
    col_block = M // N_COL
    back = jnp.zeros((M, C), jnp.float32)
    for block in range(N_COL):
        lower = block * col_block
        back = back + rounded(jnp.dot(left_basis[:, lower:lower + col_block], direction[lower:lower + col_block, :], preferred_element_type=jnp.float32))
    back = back.astype(jnp.bfloat16)
    update = jnp.dot(back, right_rows, preferred_element_type=jnp.float32).astype(jnp.bfloat16)
    left_gram = jnp.dot(grad, grad.T, preferred_element_type=jnp.float32) * (1.0 / C)
    return (update, exp_avg_new, exp_avg_sq_new, left_gram, right_gram)
```

```python
import itertools

import jax
import jax.numpy as jnp
from jax import lax
from jax.sharding import Mesh, PartitionSpec as P

M = 5120
C = 1024

first_beta = 0.9
second_beta = 0.95
epsilon = 1e-08

SIZES = {"x": 4, "core": 2, "zh": 2, "y": 4}
ROW = ("x", "core")
f32 = jnp.float32
bf16 = jnp.bfloat16


def pairs(axes, target):
    found = []
    for place in itertools.product(*[range(SIZES[a]) for a in axes]):
        there = target(*place)
        if there is None:
            continue
        src = dst = 0
        for a, s, d in zip(axes, place, there):
            src, dst = src * SIZES[a] + s, dst * SIZES[a] + d
        found.append((src, dst))
    return found


def dot(a, b, over_a, over_b):
    return lax.dot_general(
        a, b, (((over_a,), (over_b,)), ((), ())), preferred_element_type=f32
    )


def lanes(blocks):
    return jnp.concatenate([blocks[k] for k in range(blocks.shape[0])], axis=1)


def other_core(value):
    return lax.ppermute(value, "core", [(0, 1), (1, 0)])


def other_half(value):
    return lax.ppermute(value, "zh", [(0, 1), (1, 0)])


def spread(value, axis):
    return lax.all_to_all(
        jnp.broadcast_to(value[None], (4,) + value.shape), axis, 0, 0, tiled=True
    )


def left_source(core):
    def target(x, c, z, y):
        if x // 2 != z:
            return None
        return (y, core, z, 2 * (x % 2) + c)

    return pairs(("x", "core", "zh", "y"), target)


def body(grad, left_basis, right_rows, exp_avg, exp_avg_sq):
    x, core = lax.axis_index("x"), lax.axis_index("core")
    z, y = lax.axis_index("zh"), lax.axis_index("y")
    row = 2 * x + core

    moments = lax.all_gather(
        jnp.concatenate([exp_avg, exp_avg_sq], axis=0).astype(bf16), ROW, axis=0
    )

    slab = lax.dynamic_slice_in_dim(right_rows, row * 128, 128, 0)
    mine = jnp.concatenate([grad, slab], axis=0)
    far = other_half(mine)

    near_all = spread(mine, "y")
    far_all = spread(far, "y")
    first = z == 0
    whole = jnp.concatenate(
        [
            lanes(jnp.where(first, near_all, far_all)),
            lanes(jnp.where(first, far_all, near_all)),
        ],
        axis=1,
    )
    panel, basis_slab = whole[:640], whole[640:]
    basis = lax.all_gather(basis_slab, ROW, axis=0, tiled=True)

    left = dot(left_basis, panel, 0, 0).astype(bf16)
    gram = (dot(grad, panel, 0, 0) * (1.0 / M)).astype(bf16)

    def for_core(t):
        cols = []
        for k in range(4):
            at = (2 * k + t) * 128
            cols += [gram[:64, at : at + 128], gram[64:, at : at + 128]]
        return jnp.concatenate(
            [left[320 * t : 320 * t + 320], jnp.concatenate(cols, axis=1)], axis=0
        )

    low, high = for_core(0), for_core(1)
    is_low = core == 0
    summed = jnp.where(is_low, low, high).astype(f32) + other_core(
        jnp.where(is_low, high, low)
    ).astype(f32)
    summed = summed.astype(bf16)
    summed = jnp.stack([summed[:, 256 * k : 256 * k + 256] for k in range(4)])
    summed = lax.all_to_all(summed, "x", 0, 0, tiled=True).astype(f32).sum(0)
    right_gram = jnp.concatenate([summed[320:, :128], summed[320:, 128:]], axis=0)
    half = lanes(spread(summed[:320].astype(bf16), "x"))

    rotated_half = dot(half, basis, 1, 1)
    old = lax.dynamic_slice_in_dim(moments, core * 320, 320, 1)
    old_sq = lax.dynamic_slice_in_dim(moments, 640 + core * 320, 320, 1)
    new = first_beta * lanes(old).astype(f32) + (1.0 - first_beta) * rotated_half
    new_sq = (
        second_beta * lanes(old_sq).astype(f32)
        + (1.0 - second_beta) * rotated_half * rotated_half
    )
    direction = (new / (jnp.sqrt(new_sq) + epsilon)).astype(bf16)
    turned = dot(direction, basis, 1, 0).astype(bf16)
    turned_far = other_core(turned)
    basis_swapped = jnp.where(
        is_low,
        left_basis,
        jnp.concatenate([left_basis[:, 320:], left_basis[:, :320]], axis=1),
    )
    back = dot(
        basis_swapped, jnp.concatenate([turned, turned_far], axis=0), 1, 0
    ).astype(bf16)
    back = jnp.stack(
        [
            jnp.concatenate(
                [back[:, 128 * k : 128 * k + 128], back[:, 512 + 128 * k : 640 + 128 * k]], axis=0
            )
            for k in range(4)
        ]
    )
    back = lax.all_to_all(back, "y", 0, 0, tiled=True).astype(f32).sum(0)
    keep = jnp.where(first, back[:640], back[640:])
    send = jnp.where(first, back[640:], back[:640]).astype(bf16)
    update = (keep + other_half(send).astype(f32)).astype(bf16)

    own = lax.dynamic_slice_in_dim(rotated_half, row * 128, 128, 1)
    theirs = lax.dynamic_slice_in_dim(rotated_half, (2 * x + 1 - core) * 128, 128, 1)
    theirs = other_core(theirs)
    rotated = jnp.where(
        is_low,
        jnp.concatenate([own, theirs], axis=0),
        jnp.concatenate([theirs, own], axis=0),
    )
    exp_avg_new = first_beta * exp_avg + (1.0 - first_beta) * rotated
    exp_avg_sq_new = second_beta * exp_avg_sq + (1.0 - second_beta) * rotated * rotated

    piece = lax.dynamic_slice_in_dim(panel, y * 256, 256, 1)
    axes = ("x", "core", "zh", "y")
    pair = lax.ppermute(piece[:, :128], axes, left_source(0)) + lax.ppermute(
        piece[:, 128:], axes, left_source(1)
    )
    paired = lanes(lax.all_gather(pair, ROW, axis=0))
    left_gram = dot(panel, paired, 1, 1) * (1.0 / C)
    return (update, exp_avg_new, exp_avg_sq_new, left_gram, right_gram)


def solution(mesh):
    wide = Mesh(
        mesh.devices.reshape(8, 4, 2, 2, 4), ("layer", "x", "core", "zh", "y")
    )
    row, col = ("x", "core"), ("zh", "y")
    return jax.shard_map(
        body,
        mesh=wide,
        in_specs=(
            P(("layer",) + row, col),
            P(("layer",) + row, col),
            P("layer", col),
            P(("layer",) + col, row),
            P(("layer",) + col, row),
        ),
        out_specs=(
            P(("layer",) + row, col),
            P(("layer",) + col, row),
            P(("layer",) + col, row),
            P(("layer",) + row, col),
            P(("layer",) + col, row),
        ),
        check_vma=False,
    )
```

```python
import itertools

import jax
import jax.numpy as jnp
from jax import lax
from jax.experimental import pallas as pl
from jax.experimental.pallas import tpu as pltpu
from jax.sharding import Mesh, PartitionSpec as P

M = 5120
C = 1024

first_beta = 0.9
second_beta = 0.95
epsilon = 1e-08

SIZES = {"x": 4, "core": 2, "zh": 2, "y": 4}
ROW = ("x", "core")
f32 = jnp.float32
bf16 = jnp.bfloat16


def pairs(axes, target):
    found = []
    for place in itertools.product(*[range(SIZES[a]) for a in axes]):
        there = target(*place)
        if there is None:
            continue
        src = dst = 0
        for a, s, d in zip(axes, place, there):
            src, dst = src * SIZES[a] + s, dst * SIZES[a] + d
        found.append((src, dst))
    return found


def dot(a, b, over_a, over_b):
    return lax.dot_general(
        a, b, (((over_a,), (over_b,)), ((), ())), preferred_element_type=f32
    )


def other_core(value):
    return lax.ppermute(value, "core", [(0, 1), (1, 0)])


def other_half(value):
    return lax.ppermute(value, "zh", [(0, 1), (1, 0)])


def spread(value, axis):
    return lax.all_to_all(
        jnp.broadcast_to(value[None], (4,) + value.shape), axis, 0, 0, tiled=True
    )


def left_source(core):
    def target(x, c, z, y):
        if x // 2 != z:
            return None
        return (y, core, z, 2 * (x % 2) + c)

    return pairs(("x", "core", "zh", "y"), target)


def shaped(shape, dtype):
    return jax.ShapeDtypeStruct(shape, dtype)


def call(kernel, outs, where, *operands, after=(), scratch=(), flops=0, moved=0):
    n = len(operands)

    def inner(*refs):
        kernel(*refs[: n + 1], *refs[n + 1 + len(after) :])

    return pl.pallas_call(
        inner,
        out_shape=outs,
        in_specs=[pl.BlockSpec(memory_space=pltpu.SMEM)]
        + [pl.BlockSpec(memory_space=pltpu.VMEM)] * n
        + [pl.BlockSpec(memory_space=pl.ANY)] * len(after),
        scratch_shapes=scratch,
        compiler_params=pltpu.CompilerParams(vmem_limit_bytes=40 * 1024 * 1024),
        cost_estimate=pl.CostEstimate(
            flops=flops, bytes_accessed=moved, transcendentals=0
        ),
    )(where, *operands, *after)


def first_kernel(where, grad, right, mine, four):
    at = pl.multiple_of(where[0] * 128, 128)
    slab = right[pl.ds(at, 128)]
    mine[:640] = grad[...]
    mine[640:] = slab
    for k in range(4):
        four[k, :640] = grad[...]
        four[k, 640:] = slab


def four_kernel(where, value, four):
    for k in range(4):
        four[k] = value[...]


def basis_kernel(where, near, far, out):
    for k in range(4):
        out[:, 128 * k : 128 * k + 128] = near[k, 640:]
        out[:, 512 + 128 * k : 640 + 128 * k] = far[k, 640:]


def left_kernel(where, near, far, grad, left, keep, send, panel):
    core, z = where[1], where[2]
    for k in range(4):
        panel[:, 128 * k : 128 * k + 128] = near[k, :640, :]
        panel[:, 512 + 128 * k : 640 + 128 * k] = far[k, :640, :]

    product = dot(left[...], panel[...], 0, 0).astype(bf16)
    gram = (dot(grad[...], panel[...], 0, 0) * (1.0 / M)).astype(bf16)

    def columns(t, flip):
        found = []
        for k in range(4):
            block = 2 * k + t
            if flip:
                block = (block + 4) % 8
            at = block * 128
            found += [gram[:64, at : at + 128], gram[64:, at : at + 128]]
        return jnp.concatenate(found, axis=1)

    for c in range(2):

        @pl.when(core == c)
        def _():
            keep[:320] = product[320 * c : 320 * c + 320]
            send[:320] = product[320 * (1 - c) : 320 * (1 - c) + 320]
            for half in range(2):

                @pl.when(z == half)
                def _():
                    keep[320:] = columns(c, half == 1)
                    send[320:] = columns(1 - c, half == 1)


def join_kernel(where, first, second, four):
    for k in range(4):
        at = slice(256 * k, 256 * k + 256)
        four[k] = (first[:, at].astype(f32) + second[:, at].astype(f32)).astype(bf16)


def sum_kernel(where, parts, rows, gram):
    total = (
        parts[0].astype(f32)
        + parts[1].astype(f32)
        + parts[2].astype(f32)
        + parts[3].astype(f32)
    )
    mine = total[:320].astype(bf16)
    for k in range(4):
        rows[k] = mine
    gram[:64] = total[320:, :128]
    gram[64:] = total[320:, 128:]


def turn_kernel(where, half, basis, moments, out, own, theirs, rows, rotated):
    row, core = where[0], where[1]
    for k in range(4):
        rows[:, 256 * k : 256 * k + 256] = half[k]
    rotated[...] = dot(rows[...], basis[...], 1, 1)
    at = pl.multiple_of(core * 320, 320)
    for i in range(8):
        turned = rotated[:, 128 * i : 128 * i + 128]
        old = moments[i, 0, pl.ds(at, 320)].astype(f32)
        old_sq = moments[i, 1, pl.ds(at, 320)].astype(f32)
        new = first_beta * old + (1.0 - first_beta) * turned
        new_sq = second_beta * old_sq + (1.0 - second_beta) * turned * turned
        rows[:, 128 * i : 128 * i + 128] = (new / (jnp.sqrt(new_sq) + epsilon)).astype(bf16)
    out[...] = dot(rows[...], basis[...], 1, 0).astype(bf16)
    own[...] = rotated[:, pl.ds(pl.multiple_of(row * 128, 128), 128)]
    next_row = row + 1 - 2 * core
    theirs[...] = rotated[:, pl.ds(pl.multiple_of(next_row * 128, 128), 128)]


def back_kernel(where, left, mine, other, top, bottom, joined):
    core = where[1]
    joined[pl.ds(pl.multiple_of(core * 320, 320), 320)] = mine[...]
    joined[pl.ds(pl.multiple_of(320 - core * 320, 320), 320)] = other[...]
    for out, at in ((top, 0), (bottom, 320)):
        product = dot(left[at : at + 320, :], joined[...], 1, 0).astype(bf16)
        for k in range(4):
            out[k, :320] = product[:, 128 * k : 128 * k + 128]
            out[k, 320:] = product[:, 512 + 128 * k : 640 + 128 * k]


def gram_kernel(where, near, far, paired, out, panel, other):
    for k in range(4):
        panel[:, 128 * k : 128 * k + 128] = near[k, :640, :]
        panel[:, 512 + 128 * k : 640 + 128 * k] = far[k, :640, :]
    for k in range(8):
        other[:, 128 * k : 128 * k + 128] = paired[k]
    out[...] = dot(panel[...], other[...], 1, 1) * (1.0 / C)


def body(grad, left_basis, right_rows, exp_avg, exp_avg_sq):
    x, core = lax.axis_index("x"), lax.axis_index("core")
    z, y = lax.axis_index("zh"), lax.axis_index("y")
    row = 2 * x + core
    where = jnp.stack([row, core, z, y]).astype(jnp.int32)
    is_low = core == 0

    mine, four = call(
        first_kernel,
        [shaped((768, 128), bf16), shaped((4, 768, 128), bf16)],
        where,
        grad,
        right_rows,
        moved=1_500_000,
    )
    far = other_half(mine)
    near_all = lax.all_to_all(four, "y", 0, 0, tiled=True)

    moments = lax.all_gather(
        jnp.stack([exp_avg, exp_avg_sq]).astype(bf16), ROW, axis=0
    )

    far_four = call(
        four_kernel, shaped((4, 768, 128), bf16), where, far, moved=1_000_000
    )
    far_all = lax.all_to_all(far_four, "y", 0, 0, tiled=True)
    slabs = call(
        basis_kernel,
        shaped((128, 1024), bf16),
        where,
        near_all,
        far_all,
        moved=1_800_000,
    )
    basis = lax.all_gather(slabs, ROW, axis=0, tiled=True)

    keep, send = call(
        left_kernel,
        [shaped((384, 1024), bf16)] * 2,
        where,
        near_all,
        far_all,
        grad,
        left_basis,
        after=(moments,),
        scratch=[pltpu.VMEM((640, 1024), bf16)],
        flops=1_000_000_000,
        moved=5_000_000,
    )
    summed = call(
        join_kernel,
        shaped((4, 384, 256), bf16),
        where,
        keep,
        other_core(send),
        moved=2_400_000,
    )
    summed = lax.all_to_all(summed, "x", 0, 0, tiled=True)
    rows, right_gram = call(
        sum_kernel,
        [shaped((4, 320, 256), bf16), shaped((128, 128), f32)],
        where,
        summed,
        moved=1_500_000,
    )
    half = lax.all_to_all(rows, "x", 0, 0, tiled=True)

    turned, own, theirs = call(
        turn_kernel,
        [shaped((320, 1024), bf16), shaped((320, 128), f32), shaped((320, 128), f32)],
        where,
        half,
        basis,
        moments,
        scratch=[
            pltpu.VMEM((320, 1024), bf16),
            pltpu.VMEM((320, 1024), f32),
        ],
        flops=1_400_000_000,
        moved=6_000_000,
    )
    top, bottom = call(
        back_kernel,
        [shaped((4, 640, 128), bf16)] * 2,
        where,
        left_basis,
        turned,
        other_core(turned),
        scratch=[pltpu.VMEM((640, 1024), bf16)],
        flops=840_000_000,
        moved=4_000_000,
    )
    top = lax.all_to_all(top, "y", 0, 0, tiled=True)
    bottom = lax.all_to_all(bottom, "y", 0, 0, tiled=True)
    updates = []
    for part in (top, bottom):
        part = part.astype(f32).sum(0)
        arrived = other_half(part[320:].astype(bf16))
        updates.append((part[:320] + arrived.astype(f32)).astype(bf16))
    update = jnp.concatenate(updates, axis=0)

    theirs = other_core(theirs)
    rotated = jnp.where(
        is_low,
        jnp.concatenate([own, theirs], axis=0),
        jnp.concatenate([theirs, own], axis=0),
    )
    exp_avg_new = first_beta * exp_avg + (1.0 - first_beta) * rotated
    exp_avg_sq_new = second_beta * exp_avg_sq + (1.0 - second_beta) * rotated * rotated

    axes = ("x", "core", "zh", "y")
    at = 2 * (y % 2)

    def piece(t):
        return jnp.where(
            y < 2,
            lax.dynamic_index_in_dim(near_all, at + t, 0, False)[:640],
            lax.dynamic_index_in_dim(far_all, at + t, 0, False)[:640],
        )

    pair = lax.ppermute(piece(0), axes, left_source(0)) + lax.ppermute(
        piece(1), axes, left_source(1)
    )
    paired = lax.all_gather(pair, ROW, axis=0)
    left_gram = call(
        gram_kernel,
        shaped((640, 640), f32),
        where,
        near_all,
        far_all,
        paired,
        after=(bottom,),
        scratch=[pltpu.VMEM((640, 1024), bf16), pltpu.VMEM((640, 1024), bf16)],
        flops=840_000_000,
        moved=6_000_000,
    )
    return (update, exp_avg_new, exp_avg_sq_new, left_gram, right_gram)


def solution(mesh):
    wide = Mesh(
        mesh.devices.reshape(8, 4, 2, 2, 4), ("layer", "x", "core", "zh", "y")
    )
    row, col = ("x", "core"), ("zh", "y")
    return jax.shard_map(
        body,
        mesh=wide,
        in_specs=(
            P(("layer",) + row, col),
            P(("layer",) + row, col),
            P("layer", col),
            P(("layer",) + col, row),
            P(("layer",) + col, row),
        ),
        out_specs=(
            P(("layer",) + row, col),
            P(("layer",) + col, row),
            P(("layer",) + col, row),
            P(("layer",) + row, col),
            P(("layer",) + col, row),
        ),
        check_vma=False,
    )
```

```python
import itertools

import jax
import jax.numpy as jnp
from jax import lax
from jax.experimental import pallas as pl
from jax.experimental.pallas import tpu as pltpu
from jax.sharding import Mesh, PartitionSpec as P

M = 5120
C = 1024

first_beta = 0.9
second_beta = 0.95
epsilon = 1e-08

SIZES = {"x": 4, "core": 2, "zh": 2, "y": 4}
ROW = ("x", "core")
f32 = jnp.float32
bf16 = jnp.bfloat16


def pairs(axes, target):
    found = []
    for place in itertools.product(*[range(SIZES[a]) for a in axes]):
        there = target(*place)
        if there is None:
            continue
        src = dst = 0
        for a, s, d in zip(axes, place, there):
            src, dst = src * SIZES[a] + s, dst * SIZES[a] + d
        found.append((src, dst))
    return found


def dot(a, b, over_a, over_b):
    return lax.dot_general(
        a, b, (((over_a,), (over_b,)), ((), ())), preferred_element_type=f32
    )


def other_core(value):
    return lax.ppermute(value, "core", [(0, 1), (1, 0)])


def other_half(value):
    return lax.ppermute(value, "zh", [(0, 1), (1, 0)])


def spread(value, axis):
    return lax.all_to_all(
        jnp.broadcast_to(value[None], (4,) + value.shape), axis, 0, 0, tiled=True
    )


def left_source(core):
    def target(x, c, z, y):
        if x // 2 != z:
            return None
        return (y, core, z, 2 * (x % 2) + c)

    return pairs(("x", "core", "zh", "y"), target)


def shaped(shape, dtype):
    return jax.ShapeDtypeStruct(shape, dtype)


def call(
    kernel, outs, where, *operands, hbm=(), after=(), scratch=(), flops=0, moved=0, limit=40
):
    n = len(operands) + len(hbm)

    def inner(*refs):
        kernel(*refs[: n + 1], *refs[n + 1 + len(after) :])

    return pl.pallas_call(
        inner,
        out_shape=outs,
        in_specs=[pl.BlockSpec(memory_space=pltpu.SMEM)]
        + [pl.BlockSpec(memory_space=pltpu.VMEM)] * len(operands)
        + [pl.BlockSpec(memory_space=pl.ANY)] * (len(hbm) + len(after)),
        scratch_shapes=scratch,
        compiler_params=pltpu.CompilerParams(vmem_limit_bytes=limit * 1024 * 1024),
        cost_estimate=pl.CostEstimate(
            flops=flops, bytes_accessed=moved, transcendentals=0
        ),
    )(where, *operands, *hbm, *after)


def first_kernel(where, grad, right, first, second, mine, moments):
    mine[:640] = grad[...]
    mine[640:] = right[pl.ds(pl.multiple_of(where[0] * 128, 128), 128)]
    moments[0] = first[...].astype(bf16)
    moments[1] = second[...].astype(bf16)


def left_kernel(where, near, far, grad, left, keep, send, slabs, panel):
    core, z = where[1], where[2]
    for k in range(4):
        slabs[:, 128 * k : 128 * k + 128] = near[k, 640:]
        slabs[:, 512 + 128 * k : 640 + 128 * k] = far[k, 640:]
        panel[:, 128 * k : 128 * k + 128] = near[k, :640, :]
        panel[:, 512 + 128 * k : 640 + 128 * k] = far[k, :640, :]

    product = dot(left[...], panel[...], 0, 0).astype(bf16)
    gram = (dot(grad[...], panel[...], 0, 0) * (1.0 / M)).astype(bf16)

    def columns(t, flip):
        found = []
        for k in range(4):
            block = 2 * k + t
            if flip:
                block = (block + 4) % 8
            at = block * 128
            found += [gram[:64, at : at + 128], gram[64:, at : at + 128]]
        return jnp.concatenate(found, axis=1)

    for c in range(2):

        @pl.when(core == c)
        def _():
            keep[:320] = product[320 * c : 320 * c + 320]
            send[:320] = product[320 * (1 - c) : 320 * (1 - c) + 320]
            for half in range(2):

                @pl.when(z == half)
                def _():
                    keep[320:] = columns(c, half == 1)
                    send[320:] = columns(1 - c, half == 1)


def join_kernel(where, first, second, four):
    for k in range(4):
        at = slice(256 * k, 256 * k + 256)
        four[k] = (first[:, at].astype(f32) + second[:, at].astype(f32)).astype(bf16)


def sum_kernel(where, parts, rows, gram):
    total = (
        parts[0].astype(f32)
        + parts[1].astype(f32)
        + parts[2].astype(f32)
        + parts[3].astype(f32)
    )
    rows[...] = total[:320].astype(bf16)
    gram[:64] = total[320:, :128]
    gram[64:] = total[320:, 128:]


def turn_kernel(
    where, half, basis, moments, out, own, theirs, rows, rotated, right, old, sems
):
    row, core = where[0], where[1]
    copies = [
        pltpu.make_async_copy(
            basis.at[pl.ds(256 * c, 256)], right.at[pl.ds(256 * c, 256)], sems.at[c]
        )
        for c in range(4)
    ]
    at = pl.multiple_of(core * 320, 320)
    copies += [
        pltpu.make_async_copy(
            moments.at[pl.ds(4 * c, 4), :, pl.ds(at, 320)],
            old.at[pl.ds(4 * c, 4)],
            sems.at[4 + c],
        )
        for c in range(2)
    ]
    for copy in copies:
        copy.start()
    for k in range(4):
        rows[:, 256 * k : 256 * k + 256] = half[k]
    for c in range(4):
        copies[c].wait()
        rotated[:, 256 * c : 256 * c + 256] = dot(
            rows[...], right[256 * c : 256 * c + 256], 1, 1
        )
    copies[4].wait()
    copies[5].wait()
    for i in range(8):
        turned = rotated[:, 128 * i : 128 * i + 128]
        new = first_beta * old[i, 0].astype(f32) + (1.0 - first_beta) * turned
        new_sq = (
            second_beta * old[i, 1].astype(f32) + (1.0 - second_beta) * turned * turned
        )
        rows[:, 128 * i : 128 * i + 128] = (new / (jnp.sqrt(new_sq) + epsilon)).astype(bf16)
    out[...] = dot(rows[...], right[...], 1, 0).astype(bf16)
    own[...] = rotated[:, pl.ds(pl.multiple_of(row * 128, 128), 128)]
    next_row = row + 1 - 2 * core
    theirs[...] = rotated[:, pl.ds(pl.multiple_of(next_row * 128, 128), 128)]


def back_kernel(where, left, mine, other, top, bottom, joined):
    core = where[1]
    joined[pl.ds(pl.multiple_of(core * 320, 320), 320)] = mine[...]
    joined[pl.ds(pl.multiple_of(320 - core * 320, 320), 320)] = other[...]
    for out, at in ((top, 0), (bottom, 320)):
        product = dot(left[at : at + 320, :], joined[...], 1, 0).astype(bf16)
        for k in range(4):
            out[k, :320] = product[:, 128 * k : 128 * k + 128]
            out[k, 320:] = product[:, 512 + 128 * k : 640 + 128 * k]


def fold_kernel(where, parts, keep, send):
    total = (
        parts[0].astype(f32)
        + parts[1].astype(f32)
        + parts[2].astype(f32)
        + parts[3].astype(f32)
    )
    keep[...] = total[:320]
    send[...] = total[320:].astype(bf16)


def update_kernel(where, top, bottom, far_top, far_bottom, update):
    update[:320] = (top[...] + far_top[...].astype(f32)).astype(bf16)
    update[320:] = (bottom[...] + far_bottom[...].astype(f32)).astype(bf16)


def moments_kernel(where, own, theirs, first, second, first_new, second_new):
    core = where[1]
    for turned, at in ((own, core * 320), (theirs, 320 - core * 320)):
        rows = pl.ds(pl.multiple_of(at, 320), 320)
        value = turned[...]
        first_new[rows] = first_beta * first[rows] + (1.0 - first_beta) * value
        second_new[rows] = (
            second_beta * second[rows] + (1.0 - second_beta) * value * value
        )


def pair_kernel(where, first, second, out):
    out[...] = first[...] + second[...]


def gram_kernel(where, near, far, paired, out, corner, panel, other):
    for k in range(4):
        panel[:, 128 * k : 128 * k + 128] = near[k, :640, :]
        panel[:, 512 + 128 * k : 640 + 128 * k] = far[k, :640, :]
    for k in range(8):
        other[:, 128 * k : 128 * k + 128] = paired[k]
    out[...] = dot(panel[...], other[...], 1, 1) * (1.0 / C)
    corner[...] = out[:8, :128]


def body(grad, left_basis, right_rows, exp_avg, exp_avg_sq):
    x, core = lax.axis_index("x"), lax.axis_index("core")
    z, y = lax.axis_index("zh"), lax.axis_index("y")
    row = 2 * x + core
    where = jnp.stack([row, core, z, y]).astype(jnp.int32)

    mine, moments = call(
        first_kernel,
        [shaped((768, 128), bf16), shaped((2, 640, 128), bf16)],
        where,
        grad,
        right_rows,
        exp_avg,
        exp_avg_sq,
        moved=1_500_000,
    )
    far = other_half(mine)
    near_all = lax.all_gather(mine, "y", axis=0)

    moments = lax.all_gather(moments, ROW, axis=0)
    far_all = lax.all_gather(far, "y", axis=0)

    keep, send, slabs = call(
        left_kernel,
        [shaped((384, 1024), bf16)] * 2 + [shaped((128, 1024), bf16)],
        where,
        near_all,
        far_all,
        grad,
        left_basis,
        scratch=[pltpu.VMEM((640, 1024), bf16)],
        flops=1_000_000_000,
        moved=5_000_000,
    )
    basis = lax.all_gather(slabs, ROW, axis=0, tiled=True)
    summed = call(
        join_kernel,
        shaped((4, 384, 256), bf16),
        where,
        keep,
        other_core(send),
        after=(moments[:1, :1, :16],),
        moved=2_400_000,
    )
    summed = lax.all_to_all(summed, "x", 0, 0, tiled=True)
    rows, right_gram = call(
        sum_kernel,
        [shaped((320, 256), bf16), shaped((128, 128), f32)],
        where,
        summed,
        moved=1_500_000,
    )
    half = lax.all_gather(rows, "x", axis=0)

    axes = ("x", "core", "zh", "y")
    at = 2 * (y % 2)

    def piece(t):
        return jnp.where(
            y < 2,
            lax.dynamic_index_in_dim(near_all, at + t, 0, False)[:640],
            lax.dynamic_index_in_dim(far_all, at + t, 0, False)[:640],
        )

    pieces = [lax.ppermute(piece(t), axes, left_source(t)) for t in range(2)]

    turned, own, theirs = call(
        turn_kernel,
        [shaped((320, 1024), bf16), shaped((320, 128), f32), shaped((320, 128), f32)],
        where,
        half,
        hbm=(basis, moments),
        after=tuple(pieces),
        scratch=[
            pltpu.VMEM((320, 1024), bf16),
            pltpu.VMEM((320, 1024), f32),
            pltpu.VMEM((1024, 1024), bf16),
            pltpu.VMEM((8, 2, 320, 128), bf16),
            pltpu.SemaphoreType.DMA((6,)),
        ],
        limit=60,
        flops=1_400_000_000,
        moved=6_000_000,
    )
    top_parts, bottom_parts = call(
        back_kernel,
        [shaped((4, 640, 128), bf16)] * 2,
        where,
        left_basis,
        turned,
        other_core(turned),
        scratch=[pltpu.VMEM((640, 1024), bf16)],
        flops=840_000_000,
        moved=4_000_000,
    )
    top = lax.all_to_all(top_parts, "y", 0, 0, tiled=True)
    bottom = lax.all_to_all(bottom_parts, "y", 0, 0, tiled=True)
    kept, arrived = [], []
    for part in (top, bottom):
        keep, send = call(
            fold_kernel,
            [shaped((320, 128), f32), shaped((320, 128), bf16)],
            where,
            part,
            moved=1_000_000,
        )
        kept.append(keep)
        arrived.append(other_half(send))

    exp_avg_new, exp_avg_sq_new = call(
        moments_kernel,
        [shaped((640, 128), f32)] * 2,
        where,
        own,
        other_core(theirs),
        exp_avg,
        exp_avg_sq,
        after=(bottom,),
        moved=1_700_000,
    )

    pair = call(
        pair_kernel,
        shaped((640, 128), bf16),
        where,
        *pieces,
        after=(top_parts,),
        moved=500_000,
    )
    paired = lax.all_gather(pair, ROW, axis=0)
    left_gram, corner = call(
        gram_kernel,
        [shaped((640, 640), f32), shaped((8, 128), f32)],
        where,
        near_all,
        far_all,
        paired,
        after=(bottom,),
        scratch=[pltpu.VMEM((640, 1024), bf16), pltpu.VMEM((640, 1024), bf16)],
        flops=840_000_000,
        moved=6_000_000,
    )
    update = call(
        update_kernel,
        shaped((640, 128), bf16),
        where,
        *kept,
        *arrived,
        after=(corner,),
        moved=700_000,
    )
    return (update, exp_avg_new, exp_avg_sq_new, left_gram, right_gram)


def solution(mesh):
    wide = Mesh(
        mesh.devices.reshape(8, 4, 2, 2, 4), ("layer", "x", "core", "zh", "y")
    )
    row, col = ("x", "core"), ("zh", "y")
    return jax.shard_map(
        body,
        mesh=wide,
        in_specs=(
            P(("layer",) + row, col),
            P(("layer",) + row, col),
            P("layer", col),
            P(("layer",) + col, row),
            P(("layer",) + col, row),
        ),
        out_specs=(
            P(("layer",) + row, col),
            P(("layer",) + col, row),
            P(("layer",) + col, row),
            P(("layer",) + row, col),
            P(("layer",) + col, row),
        ),
        check_vma=False,
    )
```

```python
import itertools

import jax
import jax.numpy as jnp
from jax import lax
from jax.experimental import pallas as pl
from jax.experimental.pallas import tpu as pltpu
from jax.sharding import Mesh, PartitionSpec as P

M = 5120
C = 1024

first_beta = 0.9
second_beta = 0.95
epsilon = 1e-08

SIZES = {"x": 4, "core": 2, "zh": 2, "y": 4}
ROW = ("x", "core")
f32 = jnp.float32
bf16 = jnp.bfloat16


def pairs(axes, target):
    found = []
    for place in itertools.product(*[range(SIZES[a]) for a in axes]):
        there = target(*place)
        if there is None:
            continue
        src = dst = 0
        for a, s, d in zip(axes, place, there):
            src, dst = src * SIZES[a] + s, dst * SIZES[a] + d
        found.append((src, dst))
    return found


def dot(a, b, over_a, over_b):
    return lax.dot_general(
        a, b, (((over_a,), (over_b,)), ((), ())), preferred_element_type=f32
    )


def other_core(value):
    return lax.ppermute(value, "core", [(0, 1), (1, 0)])


def other_half(value):
    return lax.ppermute(value, "zh", [(0, 1), (1, 0)])


def spread(value, axis):
    return lax.all_to_all(
        jnp.broadcast_to(value[None], (4,) + value.shape), axis, 0, 0, tiled=True
    )


def left_source(core):
    def target(x, c, z, y):
        if x // 2 != z:
            return None
        return (y, core, z, 2 * (x % 2) + c)

    return pairs(("x", "core", "zh", "y"), target)


def shaped(shape, dtype):
    return jax.ShapeDtypeStruct(shape, dtype)


def call(
    kernel, outs, where, *operands, hbm=(), after=(), to_hbm=(), scratch=(), flops=0, moved=0, limit=40
):
    n = len(operands) + len(hbm)

    def inner(*refs):
        kernel(*refs[: n + 1], *refs[n + 1 + len(after) :])

    spaces = [pltpu.HBM if k in to_hbm else pltpu.VMEM for k in range(len(outs))]
    return pl.pallas_call(
        inner,
        out_shape=outs,
        in_specs=[pl.BlockSpec(memory_space=pltpu.SMEM)]
        + [pl.BlockSpec(memory_space=pltpu.VMEM)] * len(operands)
        + [pl.BlockSpec(memory_space=pltpu.HBM)] * len(hbm)
        + [pl.BlockSpec(memory_space=pl.ANY)] * len(after),
        out_specs=[pl.BlockSpec(memory_space=space) for space in spaces],
        scratch_shapes=scratch,
        compiler_params=pltpu.CompilerParams(vmem_limit_bytes=limit * 1024 * 1024),
        cost_estimate=pl.CostEstimate(
            flops=flops, bytes_accessed=moved, transcendentals=0
        ),
    )(where, *operands, *hbm, *after)


def copies_of(pairs_of, sems):
    made = [
        pltpu.make_async_copy(src, dst, sems.at[k])
        for k, (src, dst) in enumerate(pairs_of)
    ]
    for copy in made:
        copy.start()
    return made


def first_kernel(
    where, grad, right, first, second, mine, moments, values, squares, rounded, sems
):
    rows = pl.ds(pl.multiple_of(where[0] * 128, 128), 128)
    copies = copies_of(
        [
            (first, values),
            (second, squares),
            (grad, mine.at[pl.ds(0, 640)]),
            (right.at[rows], mine.at[pl.ds(640, 128)]),
        ],
        sems,
    )
    copies[0].wait()
    rounded[0] = values[...].astype(bf16)
    copies[1].wait()
    rounded[1] = squares[...].astype(bf16)
    last = pltpu.make_async_copy(rounded, moments, sems.at[4])
    last.start()
    for copy in (copies[2], copies[3], last):
        copy.wait()


def basis_kernel(where, near, out):
    for k in range(4):
        out[:, 128 * k : 128 * k + 128] = near[k, 640:]


def left_kernel(where, near, far, grad, left, keep, send, slabs, panel, leave, sems):
    core, z = where[1], where[2]
    for k in range(4):
        slabs[:, 128 * k : 128 * k + 128] = far[k, 640:]
        panel[:, 128 * k : 128 * k + 128] = near[k, :640, :]
        panel[:, 512 + 128 * k : 640 + 128 * k] = far[k, :640, :]
    gram = (dot(grad[...], panel[...], 0, 0) * (1.0 / M)).astype(bf16)

    def columns(t, flip):
        found = []
        for k in range(4):
            at = (2 * k + t + 4 * flip) % 8 * 128
            found += [gram[:64, at : at + 128], gram[64:, at : at + 128]]
        return jnp.concatenate(found, axis=1)

    for c in range(2):
        for half in range(2):

            @pl.when(jnp.logical_and(core == c, z == half))
            def _():
                keep[320:] = columns(c, half)
                leave[320:] = columns(1 - c, half)

    tail = pl.ds(320, 64)
    copies = copies_of([(leave.at[tail], send.at[tail])], sems)
    for part in range(2):
        cols = slice(512 * part, 512 * part + 512)
        product = dot(left[...], panel[:, cols], 0, 0).astype(bf16)
        for c in range(2):

            @pl.when(core == c)
            def _():
                keep[:320, cols] = product[320 * c : 320 * c + 320]
                leave[:320, cols] = product[320 * (1 - c) : 320 * (1 - c) + 320]

        block = (pl.ds(0, 320), pl.ds(512 * part, 512))
        copies += copies_of([(leave.at[block], send.at[block])], sems.at[pl.ds(1 + part, 1)])
    for copy in copies:
        copy.wait()


def join_kernel(where, first, second, four):
    for k in range(4):
        at = slice(256 * k, 256 * k + 256)
        four[k] = (first[:, at].astype(f32) + second[:, at].astype(f32)).astype(bf16)


def sum_kernel(where, parts, rows, gram, mine, sems):
    def total(at):
        return (
            parts[0, at].astype(f32)
            + parts[1, at].astype(f32)
            + parts[2, at].astype(f32)
            + parts[3, at].astype(f32)
        )

    mine[...] = total(slice(0, 320)).astype(bf16)
    copies = copies_of([(mine, rows.at[k]) for k in range(4)], sems)
    last = total(slice(320, 384))
    gram[:64] = last[:, :128]
    gram[64:] = last[:, 128:]
    for copy in copies:
        copy.wait()


def turn_kernel(
    where, half, moments, near, far, out, blocks, rows, rotated, right, sems
):
    row, core = where[0], where[1]
    copies = copies_of(
        [
            (src.at[pl.ds(512 * k, 512)], right.at[n, pl.ds(512 * k, 512)])
            for n, src in ((0, near), (1, far))
            for k in range(2)
        ],
        sems,
    )
    for k in range(4):
        rows[:, 256 * k : 256 * k + 256] = half[k]
    for k in range(2):
        copies[k].wait()
        at = slice(512 * k, 512 * k + 512)
        rotated[:, at] = dot(rows[:, :512], right[0, at], 1, 1)
    for k in range(2):
        copies[2 + k].wait()
        at = slice(512 * k, 512 * k + 512)
        rotated[:, at] += dot(rows[:, 512:], right[1, at], 1, 1)
    next_row = row + 1 - 2 * core
    for k, at in ((0, row), (1, next_row)):
        blocks[k] = rotated[:, pl.ds(pl.multiple_of(at * 128, 128), 128)]
    for i in range(8):
        turned = rotated[:, 128 * i : 128 * i + 128]
        old, old_sq = moments[i, 0].astype(f32), moments[i, 1].astype(f32)
        new = first_beta * old + (1.0 - first_beta) * turned
        new_sq = second_beta * old_sq + (1.0 - second_beta) * turned * turned
        rows[:, 128 * i : 128 * i + 128] = (new / (jnp.sqrt(new_sq) + epsilon)).astype(bf16)
    out[:, :512] = dot(rows[...], right[0], 1, 0).astype(bf16)
    out[:, 512:] = dot(rows[...], right[1], 1, 0).astype(bf16)


def back_kernel(where, left, mine, other, top, bottom, joined):
    core = where[1]
    joined[pl.ds(pl.multiple_of(core * 320, 320), 320)] = mine[...]
    joined[pl.ds(pl.multiple_of(320 - core * 320, 320), 320)] = other[...]
    for out, at in ((top, 0), (bottom, 320)):
        product = dot(left[at : at + 320, :], joined[...], 1, 0).astype(bf16)
        for k in range(4):
            out[k, :320] = product[:, 128 * k : 128 * k + 128]
            out[k, 320:] = product[:, 512 + 128 * k : 640 + 128 * k]


def fold(parts, rows):
    return (
        parts[0, rows].astype(f32)
        + parts[1, rows].astype(f32)
        + parts[2, rows].astype(f32)
        + parts[3, rows].astype(f32)
    )


def fold_kernel(where, parts, send):
    send[...] = fold(parts, slice(320, 640)).astype(bf16)


def fold_last_kernel(where, parts, blocks, send, theirs):
    send[...] = fold(parts, slice(320, 640)).astype(bf16)
    theirs[...] = blocks[1]


def update_kernel(where, kept, far_top, far_bottom, update):
    update[:320] = (kept[:320] + far_top[...].astype(f32)).astype(bf16)
    update[320:] = (kept[320:] + far_bottom[...].astype(f32)).astype(bf16)


def moments_kernel(
    where, blocks, theirs, first, second, top, bottom, first_new, second_new, kept
):
    core = where[1]
    kept[:320] = fold(top, slice(0, 320))
    kept[320:] = fold(bottom, slice(0, 320))
    for turned, at in ((blocks.at[0], core * 320), (theirs, 320 - core * 320)):
        rows = pl.ds(pl.multiple_of(at, 320), 320)
        value = turned[...]
        first_new[rows] = first_beta * first[rows] + (1.0 - first_beta) * value
        second_new[rows] = (
            second_beta * second[rows] + (1.0 - second_beta) * value * value
        )


def pair_kernel(where, first, second, out, mark):
    out[...] = first[...] + second[...]
    mark[...] = jnp.zeros_like(mark)


def gram_kernel(where, near, far, paired, out, corner, panel, other):
    for k in range(4):
        panel[:, 128 * k : 128 * k + 128] = near[k, :640, :]
        panel[:, 512 + 128 * k : 640 + 128 * k] = far[k, :640, :]
    for k in range(8):
        other[:, 128 * k : 128 * k + 128] = paired[k]
    out[...] = dot(panel[...], other[...], 1, 1) * (1.0 / C)
    corner[...] = out[:8, :128]


def body(grad, left_basis, right_rows, exp_avg, exp_avg_sq):
    x, core = lax.axis_index("x"), lax.axis_index("core")
    z, y = lax.axis_index("zh"), lax.axis_index("y")
    row = 2 * x + core
    where = jnp.stack([row, core, z, y]).astype(jnp.int32)

    mine, moments = call(
        first_kernel,
        [shaped((768, 128), bf16), shaped((2, 640, 128), bf16)],
        where,
        hbm=(grad, right_rows, exp_avg, exp_avg_sq),
        to_hbm=(0, 1),
        scratch=[
            pltpu.VMEM((640, 128), f32),
            pltpu.VMEM((640, 128), f32),
            pltpu.VMEM((2, 640, 128), bf16),
            pltpu.SemaphoreType.DMA((5,)),
        ],
        moved=1_500_000,
        limit=60,
    )
    far = other_half(mine)
    near_all = lax.all_gather(mine, "y", axis=0)

    moments = lax.all_gather(moments, ROW, axis=0)
    (basis_near,) = call(
        basis_kernel,
        [shaped((128, 512), bf16)],
        where,
        near_all,
        after=(far,),
        moved=1_000_000,
    )
    basis_near = lax.all_gather(basis_near, ROW, axis=0, tiled=True)
    far_all = lax.all_gather(far, "y", axis=0)

    keep, send, slabs = call(
        left_kernel,
        [shaped((384, 1024), bf16)] * 2 + [shaped((128, 512), bf16)],
        where,
        near_all,
        far_all,
        grad,
        left_basis,
        to_hbm=(1,),
        scratch=[
            pltpu.VMEM((640, 1024), bf16),
            pltpu.VMEM((384, 1024), bf16),
            pltpu.SemaphoreType.DMA((3,)),
        ],
        flops=1_000_000_000,
        moved=5_000_000,
    )
    basis_far = lax.all_gather(slabs, ROW, axis=0, tiled=True)
    (summed,) = call(
        join_kernel,
        [shaped((4, 384, 256), bf16)],
        where,
        keep,
        other_core(send),
        after=(moments[:1, :1, :16],),
        moved=2_400_000,
    )
    moments = lax.dynamic_slice_in_dim(moments, core * 320, 320, 2)
    summed = lax.all_to_all(summed, "x", 0, 0, tiled=True)
    rows, right_gram = call(
        sum_kernel,
        [shaped((4, 320, 256), bf16), shaped((128, 128), f32)],
        where,
        summed,
        after=(moments, basis_near[:16, :128]),
        to_hbm=(0,),
        scratch=[pltpu.VMEM((320, 256), bf16), pltpu.SemaphoreType.DMA((4,))],
        moved=1_500_000,
    )
    half = lax.all_to_all(rows, "x", 0, 0, tiled=True)

    axes = ("x", "core", "zh", "y")
    at = 2 * (y % 2)

    def piece(t):
        return jnp.where(
            y < 2,
            lax.dynamic_index_in_dim(near_all, at + t, 0, False)[:640],
            lax.dynamic_index_in_dim(far_all, at + t, 0, False)[:640],
        )

    pair, paired_mark = call(
        pair_kernel,
        [shaped((640, 128), bf16), shaped((8, 128), f32)],
        where,
        *[lax.ppermute(piece(t), axes, left_source(t)) for t in range(2)],
        moved=500_000,
    )

    turned, blocks = call(
        turn_kernel,
        [shaped((320, 1024), bf16), shaped((2, 320, 128), f32)],
        where,
        half,
        moments,
        hbm=(basis_near, basis_far),
        after=(paired_mark,),
        scratch=[
            pltpu.VMEM((320, 1024), bf16),
            pltpu.VMEM((320, 1024), f32),
            pltpu.VMEM((2, 1024, 512), bf16),
            pltpu.SemaphoreType.DMA((4,)),
        ],
        flops=1_400_000_000,
        moved=6_000_000,
    )
    turned_far = other_core(turned)
    top_parts, bottom_parts = call(
        back_kernel,
        [shaped((4, 640, 128), bf16)] * 2,
        where,
        left_basis,
        turned,
        turned_far,
        scratch=[pltpu.VMEM((640, 1024), bf16)],
        flops=840_000_000,
        moved=4_000_000,
    )
    top = lax.all_to_all(top_parts, "y", 0, 0, tiled=True)
    bottom = lax.all_to_all(bottom_parts, "y", 0, 0, tiled=True)
    (send,) = call(fold_kernel, [shaped((320, 128), bf16)], where, top, moved=700_000)
    arrived = [other_half(send)]
    send, theirs = call(
        fold_last_kernel,
        [shaped((320, 128), bf16), shaped((320, 128), f32)],
        where,
        bottom,
        blocks,
        moved=700_000,
    )
    arrived.append(other_half(send))

    exp_avg_new, exp_avg_sq_new, kept = call(
        moments_kernel,
        [shaped((640, 128), f32)] * 3,
        where,
        blocks,
        other_core(theirs),
        exp_avg,
        exp_avg_sq,
        top,
        bottom,
        moved=1_700_000,
    )

    paired = lax.all_gather(pair, ROW, axis=0)
    left_gram, corner = call(
        gram_kernel,
        [shaped((640, 640), f32), shaped((8, 128), f32)],
        where,
        near_all,
        far_all,
        paired,
        after=(bottom,),
        scratch=[pltpu.VMEM((640, 1024), bf16), pltpu.VMEM((640, 1024), bf16)],
        flops=840_000_000,
        moved=6_000_000,
    )
    (update,) = call(
        update_kernel,
        [shaped((640, 128), bf16)],
        where,
        kept,
        *arrived,
        after=(corner,),
        moved=700_000,
    )
    return (update, exp_avg_new, exp_avg_sq_new, left_gram, right_gram)


def solution(mesh):
    wide = Mesh(
        mesh.devices.reshape(8, 4, 2, 2, 4), ("layer", "x", "core", "zh", "y")
    )
    row, col = ("x", "core"), ("zh", "y")
    return jax.shard_map(
        body,
        mesh=wide,
        in_specs=(
            P(("layer",) + row, col),
            P(("layer",) + row, col),
            P("layer", col),
            P(("layer",) + col, row),
            P(("layer",) + col, row),
        ),
        out_specs=(
            P(("layer",) + row, col),
            P(("layer",) + col, row),
            P(("layer",) + col, row),
            P(("layer",) + row, col),
            P(("layer",) + col, row),
        ),
        check_vma=False,
    )
```

```python
import itertools

import jax
import jax.numpy as jnp
from jax import lax
from jax.experimental import pallas as pl
from jax.experimental.pallas import tpu as pltpu
from jax.sharding import Mesh, PartitionSpec as P

M = 5120
C = 1024

first_beta = 0.9
second_beta = 0.95
epsilon = 1e-08

SIZES = {"x": 4, "core": 2, "zh": 2, "y": 4}
ROW = ("x", "core")
f32 = jnp.float32
bf16 = jnp.bfloat16


def pairs(axes, target):
    found = []
    for place in itertools.product(*[range(SIZES[a]) for a in axes]):
        there = target(*place)
        if there is None:
            continue
        src = dst = 0
        for a, s, d in zip(axes, place, there):
            src, dst = src * SIZES[a] + s, dst * SIZES[a] + d
        found.append((src, dst))
    return found


def dot(a, b, over_a, over_b):
    return lax.dot_general(
        a, b, (((over_a,), (over_b,)), ((), ())), preferred_element_type=f32
    )


def other_core(value):
    return lax.ppermute(value, "core", [(0, 1), (1, 0)])


def other_half(value):
    return lax.ppermute(value, "zh", [(0, 1), (1, 0)])


def spread(value, axis):
    return lax.all_to_all(
        jnp.broadcast_to(value[None], (4,) + value.shape), axis, 0, 0, tiled=True
    )


def left_source(core):
    def target(x, c, z, y):
        if x // 2 != z:
            return None
        return (y, core, z, 2 * (x % 2) + c)

    return pairs(("x", "core", "zh", "y"), target)


def shaped(shape, dtype):
    return jax.ShapeDtypeStruct(shape, dtype)


def call(
    kernel, outs, where, *operands, after=(), scratch=(), flops=0, moved=0, limit=24
):
    n = len(operands)

    def inner(*refs):
        kernel(*refs[: n + 1], *refs[n + 1 + len(after) :])

    return pl.pallas_call(
        inner,
        out_shape=outs,
        in_specs=[pl.BlockSpec(memory_space=pltpu.SMEM)]
        + [pl.BlockSpec(memory_space=pltpu.VMEM)] * n
        + [pl.BlockSpec(memory_space=pl.ANY)] * len(after),
        scratch_shapes=scratch,
        compiler_params=pltpu.CompilerParams(vmem_limit_bytes=limit * 1024 * 1024),
        cost_estimate=pl.CostEstimate(
            flops=flops, bytes_accessed=moved, transcendentals=0
        ),
    )(where, *operands, *after)


def first_kernel(where, grad, right, first, second, mine, moments):
    mine[:640] = grad[...]
    mine[640:] = right[pl.ds(pl.multiple_of(where[0] * 128, 128), 128)]
    moments[0] = first[...].astype(bf16)
    moments[1] = second[...].astype(bf16)


def left_kernel(where, near, far, grad, left, keep, send, slabs, panel):
    core, z = where[1], where[2]
    for k in range(4):
        slabs[:, 128 * k : 128 * k + 128] = near[k, 640:]
        slabs[:, 512 + 128 * k : 640 + 128 * k] = far[k, 640:]
        panel[:, 128 * k : 128 * k + 128] = near[k, :640, :]
        panel[:, 512 + 128 * k : 640 + 128 * k] = far[k, :640, :]

    product = dot(left[...], panel[...], 0, 0).astype(bf16)
    gram = (dot(grad[...], panel[...], 0, 0) * (1.0 / M)).astype(bf16)

    def columns(t, flip):
        found = []
        for k in range(4):
            block = 2 * k + t
            if flip:
                block = (block + 4) % 8
            at = block * 128
            found += [gram[:64, at : at + 128], gram[64:, at : at + 128]]
        return jnp.concatenate(found, axis=1)

    for c in range(2):

        @pl.when(core == c)
        def _():
            keep[:320] = product[320 * c : 320 * c + 320]
            send[:320] = product[320 * (1 - c) : 320 * (1 - c) + 320]
            for half in range(2):

                @pl.when(z == half)
                def _():
                    keep[320:] = columns(c, half == 1)
                    send[320:] = columns(1 - c, half == 1)


def join_kernel(where, first, second, four):
    for k in range(4):
        at = slice(256 * k, 256 * k + 256)
        four[k] = (first[:, at].astype(f32) + second[:, at].astype(f32)).astype(bf16)


def sum_kernel(where, parts, rows, gram):
    total = (
        parts[0].astype(f32)
        + parts[1].astype(f32)
        + parts[2].astype(f32)
        + parts[3].astype(f32)
    )
    mine = total[:320].astype(bf16)
    for k in range(4):
        rows[k] = mine
    gram[:64] = total[320:, :128]
    gram[64:] = total[320:, 128:]


def turn_kernel(where, half, moments, basis, out, own, rows, rotated):
    row, core = where[0], where[1]
    for k in range(4):
        rows[:, 256 * k : 256 * k + 256] = half[k]
    rotated[...] = dot(rows[...], basis[...], 1, 1)
    next_row = row + 1 - 2 * core
    own[...] = rotated[:, pl.ds(pl.multiple_of(row * 128, 128), 128)]
    theirs = rotated[:, pl.ds(pl.multiple_of(next_row * 128, 128), 128)]
    out[:, 1024:] = theirs.astype(bf16)
    for i in range(8):
        turned = rotated[:, 128 * i : 128 * i + 128]
        old, old_sq = moments[i, 0].astype(f32), moments[i, 1].astype(f32)
        new = first_beta * old + (1.0 - first_beta) * turned
        new_sq = second_beta * old_sq + (1.0 - second_beta) * turned * turned
        rows[:, 128 * i : 128 * i + 128] = (new / (jnp.sqrt(new_sq) + epsilon)).astype(bf16)
    out[:, :1024] = dot(rows[...], basis[...], 1, 0).astype(bf16)


def back_kernel(where, left, mine, other, out, joined):
    core = where[1]
    joined[pl.ds(pl.multiple_of(core * 320, 320), 320)] = mine[:, :1024]
    joined[pl.ds(pl.multiple_of(320 - core * 320, 320), 320)] = other[:, :1024]
    product = dot(left[...], joined[...], 1, 0).astype(bf16)
    for k in range(4):
        out[k, :640] = product[:, 128 * k : 128 * k + 128]
        out[k, 640:] = product[:, 512 + 128 * k : 640 + 128 * k]


def fold(parts, rows):
    return (
        parts[0, rows].astype(f32)
        + parts[1, rows].astype(f32)
        + parts[2, rows].astype(f32)
        + parts[3, rows].astype(f32)
    )


def fold_kernel(where, parts, send):
    send[...] = fold(parts, slice(640, 1280)).astype(bf16)


def update_kernel(where, kept, arrived, update):
    update[...] = (kept[...] + arrived[...].astype(f32)).astype(bf16)


def moments_kernel(
    where, own, other, first, second, parts, first_new, second_new, kept
):
    core = where[1]
    kept[...] = fold(parts, slice(0, 640))
    theirs = other[:, 1024:].astype(f32)
    for value, at in ((own[...], core * 320), (theirs, 320 - core * 320)):
        rows = pl.ds(pl.multiple_of(at, 320), 320)
        first_new[rows] = first_beta * first[rows] + (1.0 - first_beta) * value
        second_new[rows] = (
            second_beta * second[rows] + (1.0 - second_beta) * value * value
        )


def pair_kernel(where, first, second, out, mark):
    out[...] = first[...] + second[...]
    mark[...] = jnp.zeros_like(mark)


def gram_kernel(where, near, far, paired, out, panel, other):
    for k in range(4):
        panel[:, 128 * k : 128 * k + 128] = near[k, :640, :]
        panel[:, 512 + 128 * k : 640 + 128 * k] = far[k, :640, :]
    for k in range(8):
        other[:, 128 * k : 128 * k + 128] = paired[k]
    out[...] = dot(panel[...], other[...], 1, 1) * (1.0 / C)


def body(grad, left_basis, right_rows, exp_avg, exp_avg_sq):
    x, core = lax.axis_index("x"), lax.axis_index("core")
    z, y = lax.axis_index("zh"), lax.axis_index("y")
    row = 2 * x + core
    where = jnp.stack([row, core, z, y]).astype(jnp.int32)

    mine, moments = call(
        first_kernel,
        [shaped((768, 128), bf16), shaped((2, 640, 128), bf16)],
        where,
        grad,
        right_rows,
        exp_avg,
        exp_avg_sq,
        moved=1_500_000,
        limit=60,
    )
    far = other_half(mine)
    near_all = lax.all_gather(mine, "y", axis=0)

    moments = lax.all_gather(moments, ROW, axis=0)
    far_all = lax.all_gather(far, "y", axis=0)

    keep, send, slabs = call(
        left_kernel,
        [shaped((384, 1024), bf16)] * 2 + [shaped((128, 1024), bf16)],
        where,
        near_all,
        far_all,
        grad,
        left_basis,
        scratch=[pltpu.VMEM((640, 1024), bf16)],
        flops=1_000_000_000,
        moved=5_000_000,
    )
    basis = lax.all_gather(slabs, ROW, axis=0, tiled=True)
    (summed,) = call(
        join_kernel,
        [shaped((4, 384, 256), bf16)],
        where,
        keep,
        other_core(send),
        after=(moments[:1, :1, :16],),
        moved=2_400_000,
    )
    moments = lax.dynamic_slice_in_dim(moments, core * 320, 320, 2)
    summed = lax.all_to_all(summed, "x", 0, 0, tiled=True)

    axes = ("x", "core", "zh", "y")
    at = 2 * (y % 2)

    def piece(t):
        return jnp.where(
            y < 2,
            lax.dynamic_index_in_dim(near_all, at + t, 0, False)[:640],
            lax.dynamic_index_in_dim(far_all, at + t, 0, False)[:640],
        )

    pair, paired_mark = call(
        pair_kernel,
        [shaped((640, 128), bf16), shaped((8, 128), f32)],
        where,
        *[lax.ppermute(piece(t), axes, left_source(t)) for t in range(2)],
        moved=500_000,
    )

    rows, right_gram = call(
        sum_kernel,
        [shaped((4, 320, 256), bf16), shaped((128, 128), f32)],
        where,
        summed,
        after=(moments[:1, :1, :16], paired_mark),
        moved=1_500_000,
    )
    half = lax.all_to_all(rows, "x", 0, 0, tiled=True)

    turned, own = call(
        turn_kernel,
        [shaped((320, 1152), bf16), shaped((320, 128), f32)],
        where,
        half,
        moments,
        basis,
        scratch=[pltpu.VMEM((320, 1024), bf16), pltpu.VMEM((320, 1024), f32)],
        flops=1_400_000_000,
        moved=6_000_000,
    )
    turned_far = other_core(turned)
    (parts,) = call(
        back_kernel,
        [shaped((4, 1280, 128), bf16)],
        where,
        left_basis,
        turned,
        turned_far,
        scratch=[pltpu.VMEM((640, 1024), bf16)],
        flops=840_000_000,
        moved=4_000_000,
    )
    parts = lax.all_to_all(parts, "y", 0, 0, tiled=True)
    (send,) = call(
        fold_kernel, [shaped((640, 128), bf16)], where, parts, moved=1_400_000
    )
    arrived = other_half(send)

    paired = lax.all_gather(pair, ROW, axis=0)
    (left_gram,) = call(
        gram_kernel,
        [shaped((640, 640), f32)],
        where,
        near_all,
        far_all,
        paired,
        after=(send,),
        scratch=[pltpu.VMEM((640, 1024), bf16), pltpu.VMEM((640, 1024), bf16)],
        flops=10_000,
        moved=10_000,
    )
    exp_avg_new, exp_avg_sq_new, kept = call(
        moments_kernel,
        [shaped((640, 128), f32)] * 3,
        where,
        own,
        turned_far,
        exp_avg,
        exp_avg_sq,
        parts,
        moved=10_000,
    )

    (update,) = call(
        update_kernel,
        [shaped((640, 128), bf16)],
        where,
        kept,
        arrived,
        moved=700_000,
    )
    return (update, exp_avg_new, exp_avg_sq_new, left_gram, right_gram)


def solution(mesh):
    wide = Mesh(
        mesh.devices.reshape(8, 4, 2, 2, 4), ("layer", "x", "core", "zh", "y")
    )
    row, col = ("x", "core"), ("zh", "y")
    return jax.shard_map(
        body,
        mesh=wide,
        in_specs=(
            P(("layer",) + row, col),
            P(("layer",) + row, col),
            P("layer", col),
            P(("layer",) + col, row),
            P(("layer",) + col, row),
        ),
        out_specs=(
            P(("layer",) + row, col),
            P(("layer",) + col, row),
            P(("layer",) + col, row),
            P(("layer",) + row, col),
            P(("layer",) + col, row),
        ),
        check_vma=False,
    )
```

```python
import itertools

import jax
import jax.numpy as jnp
from jax import lax
from jax.experimental import pallas as pl
from jax.experimental.pallas import tpu as pltpu
from jax.sharding import Mesh, PartitionSpec as P

M = 5120
C = 1024

first_beta = 0.9
second_beta = 0.95
epsilon = 1e-08

SIZES = {"x": 4, "core": 2, "zh": 2, "y": 4}
ROW = ("x", "core")
f32 = jnp.float32
bf16 = jnp.bfloat16


def pairs(axes, target):
    found = []
    for place in itertools.product(*[range(SIZES[a]) for a in axes]):
        there = target(*place)
        if there is None:
            continue
        src = dst = 0
        for a, s, d in zip(axes, place, there):
            src, dst = src * SIZES[a] + s, dst * SIZES[a] + d
        found.append((src, dst))
    return found


def dot(a, b, over_a, over_b):
    return lax.dot_general(
        a, b, (((over_a,), (over_b,)), ((), ())), preferred_element_type=f32
    )


def other_core(value):
    return lax.ppermute(value, "core", [(0, 1), (1, 0)])


def other_half(value):
    axes = ("core", "zh", "y")
    return lax.ppermute(
        value, axes, pairs(axes, lambda c, z, y: (c, 1 - z, (y + 2 * c) % 4))
    )


def shifted(k, core):
    return lax.rem(k + 2 * core, 4)


def spread(value, axis):
    return lax.all_to_all(
        jnp.broadcast_to(value[None], (4,) + value.shape), axis, 0, 0, tiled=True
    )


def left_source(core):
    def target(x, c, z, y):
        if x // 2 != z:
            return None
        there = 2 * (x % 2) + c
        return ((y - there) % 4, core, z, there)

    return pairs(("x", "core", "zh", "y"), target)


def shaped(shape, dtype):
    return jax.ShapeDtypeStruct(shape, dtype)


def call(
    kernel, outs, where, *operands, after=(), scratch=(), flops=0, moved=0, limit=24
):
    n = len(operands)

    def inner(*refs):
        kernel(*refs[: n + 1], *refs[n + 1 + len(after) :])

    return pl.pallas_call(
        inner,
        out_shape=outs,
        in_specs=[pl.BlockSpec(memory_space=pltpu.SMEM)]
        + [pl.BlockSpec(memory_space=pltpu.VMEM)] * n
        + [pl.BlockSpec(memory_space=pl.ANY)] * len(after),
        scratch_shapes=scratch,
        compiler_params=pltpu.CompilerParams(vmem_limit_bytes=limit * 1024 * 1024),
        cost_estimate=pl.CostEstimate(
            flops=flops, bytes_accessed=moved, transcendentals=0
        ),
    )(where, *operands, *after)


def first_kernel(where, grad, right, first, second, mine, moments):
    mine[:640] = grad[...]
    mine[640:] = right[pl.ds(pl.multiple_of(where[0] * 128, 128), 128)]
    moments[0] = first[...].astype(bf16)
    moments[1] = second[...].astype(bf16)


def left_kernel(where, near, far, grad, left, keep, send, slabs, panel):
    core, z = where[1], where[2]
    for k in range(4):
        place = shifted(k, core)
        slabs[:, 128 * k : 128 * k + 128] = near[k, 640:]
        slabs[:, 512 + 128 * k : 640 + 128 * k] = far[place, 640:]
        panel[:, 128 * k : 128 * k + 128] = near[k, :640]
        panel[:, 512 + 128 * k : 640 + 128 * k] = far[place, :640]

    product = dot(left[...], panel[...], 0, 0).astype(bf16)
    gram = (dot(grad[...], panel[...], 0, 0) * (1.0 / M)).astype(bf16)

    def columns(t, flip):
        found = []
        for k in range(4):
            block = 2 * k + t
            if flip:
                block = (block + 4) % 8
            at = block * 128
            found += [gram[:64, at : at + 128], gram[64:, at : at + 128]]
        return jnp.concatenate(found, axis=1)

    for c in range(2):

        @pl.when(core == c)
        def _():
            keep[:320] = product[320 * c : 320 * c + 320]
            send[:320] = product[320 * (1 - c) : 320 * (1 - c) + 320]
            for half in range(2):

                @pl.when(z == half)
                def _():
                    keep[320:] = columns(c, half == 1)
                    send[320:] = columns(1 - c, half == 1)


def join_kernel(where, first, second, four):
    for k in range(4):
        at = slice(256 * k, 256 * k + 256)
        four[k] = (first[:, at].astype(f32) + second[:, at].astype(f32)).astype(bf16)


def sum_kernel(where, parts, rows, gram):
    total = (
        parts[0].astype(f32)
        + parts[1].astype(f32)
        + parts[2].astype(f32)
        + parts[3].astype(f32)
    )
    mine = total[:320].astype(bf16)
    for k in range(4):
        rows[k] = mine
    gram[:64] = total[320:, :128]
    gram[64:] = total[320:, 128:]


def turn_kernel(where, half, moments, basis, out, own, rows, rotated):
    row, core = where[0], where[1]
    for k in range(4):
        rows[:, 256 * k : 256 * k + 256] = half[k]
    rotated[...] = dot(rows[...], basis[...], 1, 1)
    next_row = row + 1 - 2 * core
    own[...] = rotated[:, pl.ds(pl.multiple_of(row * 128, 128), 128)]
    theirs = rotated[:, pl.ds(pl.multiple_of(next_row * 128, 128), 128)]
    out[:, 1024:] = theirs.astype(bf16)
    for i in range(8):
        turned = rotated[:, 128 * i : 128 * i + 128]
        old, old_sq = moments[i, 0].astype(f32), moments[i, 1].astype(f32)
        new = first_beta * old + (1.0 - first_beta) * turned
        new_sq = second_beta * old_sq + (1.0 - second_beta) * turned * turned
        rows[:, 128 * i : 128 * i + 128] = (new / (jnp.sqrt(new_sq) + epsilon)).astype(bf16)
    out[:, :1024] = dot(rows[...], basis[...], 1, 0).astype(bf16)


def back_kernel(where, left, mine, other, out, joined):
    core = where[1]
    joined[pl.ds(pl.multiple_of(core * 320, 320), 320)] = mine[:, :1024]
    joined[pl.ds(pl.multiple_of(320 - core * 320, 320), 320)] = other[:, :1024]
    product = dot(left[...], joined[...], 1, 0).astype(bf16)
    for k in range(4):
        out[k, :640] = product[:, 128 * k : 128 * k + 128]
    for c in range(2):

        @pl.when(core == c)
        def _():
            for k in range(4):
                at = 512 + 128 * ((k + 2 * c) % 4)
                out[k, 640:] = product[:, at : at + 128]


def fold(parts, rows):
    return (
        parts[0, rows].astype(f32)
        + parts[1, rows].astype(f32)
        + parts[2, rows].astype(f32)
        + parts[3, rows].astype(f32)
    )


def fold_kernel(where, parts, send):
    send[...] = fold(parts, slice(640, 1280)).astype(bf16)


def update_kernel(where, kept, arrived, update):
    update[...] = (kept[...] + arrived[...].astype(f32)).astype(bf16)


def moments_kernel(
    where, own, other, first, second, parts, first_new, second_new, kept
):
    core = where[1]
    kept[...] = fold(parts, slice(0, 640))
    theirs = other[:, 1024:].astype(f32)
    for value, at in ((own[...], core * 320), (theirs, 320 - core * 320)):
        rows = pl.ds(pl.multiple_of(at, 320), 320)
        first_new[rows] = first_beta * first[rows] + (1.0 - first_beta) * value
        second_new[rows] = (
            second_beta * second[rows] + (1.0 - second_beta) * value * value
        )


def pair_kernel(where, first, second, out, mark):
    out[...] = first[...] + second[...]
    mark[...] = jnp.zeros_like(mark)


def gram_kernel(where, near, far, paired, out, panel, other):
    for k in range(4):
        panel[:, 128 * k : 128 * k + 128] = near[k, :640]
        panel[:, 512 + 128 * k : 640 + 128 * k] = far[shifted(k, where[1]), :640]
    for k in range(8):
        other[:, 128 * k : 128 * k + 128] = paired[k]
    out[...] = dot(panel[...], other[...], 1, 1) * (1.0 / C)


def body(grad, left_basis, right_rows, exp_avg, exp_avg_sq):
    x, core = lax.axis_index("x"), lax.axis_index("core")
    z, y = lax.axis_index("zh"), lax.axis_index("y")
    row = 2 * x + core
    where = jnp.stack([row, core, z, y]).astype(jnp.int32)

    mine, moments = call(
        first_kernel,
        [shaped((768, 128), bf16), shaped((2, 640, 128), bf16)],
        where,
        grad,
        right_rows,
        exp_avg,
        exp_avg_sq,
        moved=1_500_000,
        limit=60,
    )
    far = other_half(mine)
    near_all = lax.all_gather(mine, "y", axis=0)

    moments = lax.all_gather(moments, ROW, axis=0)
    far_all = lax.all_gather(far, "y", axis=0)

    keep, send, slabs = call(
        left_kernel,
        [shaped((384, 1024), bf16)] * 2 + [shaped((128, 1024), bf16)],
        where,
        near_all,
        far_all,
        grad,
        left_basis,
        scratch=[pltpu.VMEM((640, 1024), bf16)],
        flops=1_000_000_000,
        moved=5_000_000,
    )
    basis = lax.all_gather(slabs, ROW, axis=0, tiled=True)
    (summed,) = call(
        join_kernel,
        [shaped((4, 384, 256), bf16)],
        where,
        keep,
        other_core(send),
        after=(moments[:1, :1, :16],),
        moved=2_400_000,
    )
    moments = lax.dynamic_slice_in_dim(moments, core * 320, 320, 2)
    summed = lax.all_to_all(summed, "x", 0, 0, tiled=True)

    axes = ("x", "core", "zh", "y")
    to_x = (y + 8 - 2 * (x % 2) - core) % 4
    at = 2 * (to_x % 2)

    def piece(t):
        return jnp.where(
            to_x < 2,
            lax.dynamic_index_in_dim(near_all, at + t, 0, False)[:640],
            lax.dynamic_index_in_dim(far_all, shifted(at + t, core), 0, False)[:640],
        )

    pair, paired_mark = call(
        pair_kernel,
        [shaped((640, 128), bf16), shaped((8, 128), f32)],
        where,
        *[lax.ppermute(piece(t), axes, left_source(t)) for t in range(2)],
        moved=500_000,
    )

    rows, right_gram = call(
        sum_kernel,
        [shaped((4, 320, 256), bf16), shaped((128, 128), f32)],
        where,
        summed,
        after=(moments[:1, :1, :16], paired_mark),
        moved=1_500_000,
    )
    half = lax.all_to_all(rows, "x", 0, 0, tiled=True)

    turned, own = call(
        turn_kernel,
        [shaped((320, 1152), bf16), shaped((320, 128), f32)],
        where,
        half,
        moments,
        basis,
        scratch=[pltpu.VMEM((320, 1024), bf16), pltpu.VMEM((320, 1024), f32)],
        flops=1_400_000_000,
        moved=6_000_000,
    )
    turned_far = other_core(turned)
    (parts,) = call(
        back_kernel,
        [shaped((4, 1280, 128), bf16)],
        where,
        left_basis,
        turned,
        turned_far,
        scratch=[pltpu.VMEM((640, 1024), bf16)],
        flops=840_000_000,
        moved=4_000_000,
    )
    parts = lax.all_to_all(parts, "y", 0, 0, tiled=True)
    (send,) = call(
        fold_kernel, [shaped((640, 128), bf16)], where, parts, moved=1_400_000
    )
    arrived = other_half(send)

    paired = lax.all_gather(pair, ROW, axis=0)
    (left_gram,) = call(
        gram_kernel,
        [shaped((640, 640), f32)],
        where,
        near_all,
        far_all,
        paired,
        after=(send,),
        scratch=[pltpu.VMEM((640, 1024), bf16), pltpu.VMEM((640, 1024), bf16)],
        flops=10_000,
        moved=10_000,
    )
    exp_avg_new, exp_avg_sq_new, kept = call(
        moments_kernel,
        [shaped((640, 128), f32)] * 3,
        where,
        own,
        turned_far,
        exp_avg,
        exp_avg_sq,
        parts,
        moved=10_000,
    )

    (update,) = call(
        update_kernel,
        [shaped((640, 128), bf16)],
        where,
        kept,
        arrived,
        moved=700_000,
    )
    return (update, exp_avg_new, exp_avg_sq_new, left_gram, right_gram)


def solution(mesh):
    wide = Mesh(
        mesh.devices.reshape(8, 4, 2, 2, 4), ("layer", "x", "core", "zh", "y")
    )
    row, col = ("x", "core"), ("zh", "y")
    return jax.shard_map(
        body,
        mesh=wide,
        in_specs=(
            P(("layer",) + row, col),
            P(("layer",) + row, col),
            P("layer", col),
            P(("layer",) + col, row),
            P(("layer",) + col, row),
        ),
        out_specs=(
            P(("layer",) + row, col),
            P(("layer",) + col, row),
            P(("layer",) + col, row),
            P(("layer",) + row, col),
            P(("layer",) + col, row),
        ),
        check_vma=False,
    )
```

```python
import itertools

import jax
import jax.numpy as jnp
from jax import lax
from jax.experimental import pallas as pl
from jax.experimental.pallas import tpu as pltpu
from jax.sharding import Mesh, PartitionSpec as P

M = 5120
C = 1024

first_beta = 0.9
second_beta = 0.95
epsilon = 1e-08

SIZES = {"x": 4, "core": 2, "zh": 2, "y": 4}
ROW = ("x", "core")
f32 = jnp.float32
bf16 = jnp.bfloat16


def pairs(axes, target):
    found = []
    for place in itertools.product(*[range(SIZES[a]) for a in axes]):
        there = target(*place)
        if there is None:
            continue
        src = dst = 0
        for a, s, d in zip(axes, place, there):
            src, dst = src * SIZES[a] + s, dst * SIZES[a] + d
        found.append((src, dst))
    return found


def dot(a, b, over_a, over_b):
    return lax.dot_general(
        a, b, (((over_a,), (over_b,)), ((), ())), preferred_element_type=f32
    )


def other_core(value):
    return lax.ppermute(value, "core", [(0, 1), (1, 0)])


def other_half(value):
    return lax.ppermute(value, "zh", [(0, 1), (1, 0)])


def spread(value, axis):
    return lax.all_to_all(
        jnp.broadcast_to(value[None], (4,) + value.shape), axis, 0, 0, tiled=True
    )


def left_source(core):
    def target(x, c, z, y):
        if x // 2 != z:
            return None
        there = 2 * (x % 2) + c
        return ((y - there) % 4, core, z, there)

    return pairs(("x", "core", "zh", "y"), target)


def shaped(shape, dtype):
    return jax.ShapeDtypeStruct(shape, dtype)


def call(
    kernel, outs, where, *operands, after=(), scratch=(), flops=0, moved=0, limit=16
):
    n = len(operands)

    def inner(*refs):
        kernel(*refs[: n + 1], *refs[n + 1 + len(after) :])

    return pl.pallas_call(
        inner,
        out_shape=outs,
        in_specs=[pl.BlockSpec(memory_space=pltpu.SMEM)]
        + [pl.BlockSpec(memory_space=pltpu.VMEM)] * n
        + [pl.BlockSpec(memory_space=pl.ANY)] * len(after),
        scratch_shapes=scratch,
        compiler_params=pltpu.CompilerParams(vmem_limit_bytes=limit * 1024 * 1024),
        cost_estimate=pl.CostEstimate(
            flops=flops, bytes_accessed=moved, transcendentals=0
        ),
    )(where, *operands, *after)


def first_kernel(where, grad, right, first, second, mine, moments):
    mine[:640] = grad[...]
    mine[640:] = right[pl.ds(pl.multiple_of(where[0] * 128, 128), 128)]
    moments[0] = first[...].astype(bf16)
    moments[1] = second[...].astype(bf16)


def left_kernel(where, near, far, grad, left, keep, send, slabs, panel):
    core, z = where[1], where[2]
    for k in range(4):
        slabs[:, 128 * k : 128 * k + 128] = near[k, 640:]
        slabs[:, 512 + 128 * k : 640 + 128 * k] = far[k, 640:]
        panel[:, 128 * k : 128 * k + 128] = near[k, :640]
        panel[:, 512 + 128 * k : 640 + 128 * k] = far[k, :640]

    product = dot(left[...], panel[...], 0, 0).astype(bf16)
    gram = (dot(grad[...], panel[...], 0, 0) * (1.0 / M)).astype(bf16)

    def columns(t, flip):
        found = []
        for k in range(4):
            block = 2 * k + t
            if flip:
                block = (block + 4) % 8
            at = block * 128
            found += [gram[:64, at : at + 128], gram[64:, at : at + 128]]
        return jnp.concatenate(found, axis=1)

    for c in range(2):

        @pl.when(core == c)
        def _():
            keep[:320] = product[320 * c : 320 * c + 320]
            send[:320] = product[320 * (1 - c) : 320 * (1 - c) + 320]
            for half in range(2):

                @pl.when(z == half)
                def _():
                    keep[320:] = columns(c, half == 1)
                    send[320:] = columns(1 - c, half == 1)


def join_kernel(where, first, second, four):
    for k in range(4):
        at = slice(256 * k, 256 * k + 256)
        four[k] = (first[:, at].astype(f32) + second[:, at].astype(f32)).astype(bf16)


def sum_kernel(where, parts, rows, gram):
    total = (
        parts[0].astype(f32)
        + parts[1].astype(f32)
        + parts[2].astype(f32)
        + parts[3].astype(f32)
    )
    mine = total[:320].astype(bf16)
    for k in range(4):
        rows[k] = mine
    gram[:64] = total[320:, :128]
    gram[64:] = total[320:, 128:]


def turn_kernel(where, half, moments, basis, out, own, rows, rotated):
    row, core = where[0], where[1]
    for k in range(4):
        rows[:, 256 * k : 256 * k + 256] = half[k]
    rotated[...] = dot(rows[...], basis[...], 1, 1)
    next_row = row + 1 - 2 * core
    own[...] = rotated[:, pl.ds(pl.multiple_of(row * 128, 128), 128)]
    theirs = rotated[:, pl.ds(pl.multiple_of(next_row * 128, 128), 128)]
    out[:, 1024:] = theirs.astype(bf16)
    for i in range(8):
        turned = rotated[:, 128 * i : 128 * i + 128]
        old, old_sq = moments[i, 0].astype(f32), moments[i, 1].astype(f32)
        new = first_beta * old + (1.0 - first_beta) * turned
        new_sq = second_beta * old_sq + (1.0 - second_beta) * turned * turned
        rows[:, 128 * i : 128 * i + 128] = (new / (jnp.sqrt(new_sq) + epsilon)).astype(bf16)
    out[:, :1024] = dot(rows[...], basis[...], 1, 0).astype(bf16)


def back_kernel(where, left, mine, other, out, joined):
    core = where[1]
    joined[pl.ds(pl.multiple_of(core * 320, 320), 320)] = mine[:, :1024]
    joined[pl.ds(pl.multiple_of(320 - core * 320, 320), 320)] = other[:, :1024]
    product = dot(left[...], joined[...], 1, 0).astype(bf16)
    for k in range(4):
        out[k, :640] = product[:, 128 * k : 128 * k + 128]
        out[k, 640:] = product[:, 512 + 128 * k : 640 + 128 * k]


def fold(parts, rows):
    return (
        parts[0, rows].astype(f32)
        + parts[1, rows].astype(f32)
        + parts[2, rows].astype(f32)
        + parts[3, rows].astype(f32)
    )


def fold_kernel(where, parts, send):
    send[...] = fold(parts, slice(640, 1280)).astype(bf16)


def moments_kernel(
    where, own, other, first, second, parts, first_new, second_new, kept
):
    core = where[1]
    kept[...] = fold(parts, slice(0, 640))
    theirs = other[:, 1024:].astype(f32)
    for value, at in ((own[...], core * 320), (theirs, 320 - core * 320)):
        rows = pl.ds(pl.multiple_of(at, 320), 320)
        first_new[rows] = first_beta * first[rows] + (1.0 - first_beta) * value
        second_new[rows] = (
            second_beta * second[rows] + (1.0 - second_beta) * value * value
        )


def pair_kernel(where, first, second, out, mark):
    out[...] = first[...] + second[...]
    mark[...] = jnp.zeros_like(mark)


def gram_kernel(where, near, far, paired, out, panel, other):
    for k in range(4):
        panel[:, 128 * k : 128 * k + 128] = near[k, :640]
        panel[:, 512 + 128 * k : 640 + 128 * k] = far[k, :640]
    for k in range(8):
        other[:, 128 * k : 128 * k + 128] = paired[k]
    out[...] = dot(panel[...], other[...], 1, 1) * (1.0 / C)


def body(grad, left_basis, right_rows, exp_avg, exp_avg_sq):
    x, core = lax.axis_index("x"), lax.axis_index("core")
    z, y = lax.axis_index("zh"), lax.axis_index("y")
    row = 2 * x + core
    where = jnp.stack([row, core, z, y]).astype(jnp.int32)

    mine, moments = call(
        first_kernel,
        [shaped((768, 128), bf16), shaped((2, 640, 128), bf16)],
        where,
        grad,
        right_rows,
        exp_avg,
        exp_avg_sq,
        moved=1_500_000,
        limit=60,
    )
    far = other_half(mine)
    near_all = lax.all_gather(mine, "y", axis=0)

    moments = lax.all_gather(moments, ROW, axis=0)
    far_all = lax.all_gather(far, "y", axis=0)

    keep, send, slabs = call(
        left_kernel,
        [shaped((384, 1024), bf16)] * 2 + [shaped((128, 1024), bf16)],
        where,
        near_all,
        far_all,
        grad,
        left_basis,
        scratch=[pltpu.VMEM((640, 1024), bf16)],
        flops=1_000_000_000,
        moved=5_000_000,
    )
    basis = lax.all_gather(slabs, ROW, axis=0, tiled=True)
    (summed,) = call(
        join_kernel,
        [shaped((4, 384, 256), bf16)],
        where,
        keep,
        other_core(send),
        after=(moments[:1, :1, :16],),
        moved=2_400_000,
    )
    moments = lax.dynamic_slice_in_dim(moments, core * 320, 320, 2)
    summed = lax.all_to_all(summed, "x", 0, 0, tiled=True)

    axes = ("x", "core", "zh", "y")
    to_x = (y + 8 - 2 * (x % 2) - core) % 4
    at = 2 * (to_x % 2)

    def piece(t):
        return jnp.where(
            to_x < 2,
            lax.dynamic_index_in_dim(near_all, at + t, 0, False)[:640],
            lax.dynamic_index_in_dim(far_all, at + t, 0, False)[:640],
        )

    pair, paired_mark = call(
        pair_kernel,
        [shaped((640, 128), bf16), shaped((8, 128), f32)],
        where,
        *[lax.ppermute(piece(t), axes, left_source(t)) for t in range(2)],
        moved=500_000,
    )

    rows, right_gram = call(
        sum_kernel,
        [shaped((4, 320, 256), bf16), shaped((128, 128), f32)],
        where,
        summed,
        after=(moments[:1, :1, :16],),
        moved=1_500_000,
    )
    half = lax.all_to_all(rows, "x", 0, 0, tiled=True)

    turned, own = call(
        turn_kernel,
        [shaped((320, 1152), bf16), shaped((320, 128), f32)],
        where,
        half,
        moments,
        basis,
        after=(paired_mark,),
        scratch=[pltpu.VMEM((320, 1024), bf16), pltpu.VMEM((320, 1024), f32)],
        flops=1_400_000_000,
        moved=6_000_000,
    )
    turned_far = other_core(turned)
    (parts,) = call(
        back_kernel,
        [shaped((4, 1280, 128), bf16)],
        where,
        left_basis,
        turned,
        turned_far,
        scratch=[pltpu.VMEM((640, 1024), bf16)],
        flops=840_000_000,
        moved=4_000_000,
    )
    parts = lax.all_to_all(parts, "y", 0, 0, tiled=True)
    (send,) = call(
        fold_kernel, [shaped((640, 128), bf16)], where, parts, moved=1_400_000
    )
    arrived = other_half(send)

    paired = lax.all_gather(pair, ROW, axis=0)
    (left_gram,) = call(
        gram_kernel,
        [shaped((640, 640), f32)],
        where,
        near_all,
        far_all,
        paired,
        after=(send,),
        scratch=[pltpu.VMEM((640, 1024), bf16), pltpu.VMEM((640, 1024), bf16)],
        flops=10_000,
        moved=10_000,
    )
    exp_avg_new, exp_avg_sq_new, kept = call(
        moments_kernel,
        [shaped((640, 128), f32)] * 3,
        where,
        own,
        turned_far,
        exp_avg,
        exp_avg_sq,
        parts,
        moved=10_000,
    )

    update = (kept + arrived.astype(f32)).astype(bf16)
    return (update, exp_avg_new, exp_avg_sq_new, left_gram, right_gram)


def solution(mesh):
    wide = Mesh(
        mesh.devices.reshape(8, 4, 2, 2, 4), ("layer", "x", "core", "zh", "y")
    )
    row, col = ("x", "core"), ("zh", "y")
    return jax.shard_map(
        body,
        mesh=wide,
        in_specs=(
            P(("layer",) + row, col),
            P(("layer",) + row, col),
            P("layer", col),
            P(("layer",) + col, row),
            P(("layer",) + col, row),
        ),
        out_specs=(
            P(("layer",) + row, col),
            P(("layer",) + col, row),
            P(("layer",) + col, row),
            P(("layer",) + row, col),
            P(("layer",) + col, row),
        ),
        check_vma=False,
    )
```

```python
import itertools

import jax
import jax.numpy as jnp
from jax import lax
from jax.experimental import pallas as pl
from jax.experimental.pallas import tpu as pltpu
from jax.sharding import Mesh, PartitionSpec as P

M = 5120
C = 1024

first_beta = 0.9
second_beta = 0.95
epsilon = 1e-08

SIZES = {"x": 4, "core": 2, "zh": 2, "y": 4}
ROW = ("x", "core")
f32 = jnp.float32
bf16 = jnp.bfloat16


def pairs(axes, target):
    found = []
    for place in itertools.product(*[range(SIZES[a]) for a in axes]):
        there = target(*place)
        if there is None:
            continue
        src = dst = 0
        for a, s, d in zip(axes, place, there):
            src, dst = src * SIZES[a] + s, dst * SIZES[a] + d
        found.append((src, dst))
    return found


def dot(a, b, over_a, over_b):
    return lax.dot_general(
        a, b, (((over_a,), (over_b,)), ((), ())), preferred_element_type=f32
    )


def other_core(value):
    return lax.ppermute(value, "core", [(0, 1), (1, 0)])


def other_half(value):
    return lax.ppermute(value, "zh", [(0, 1), (1, 0)])


def spread(value, axis):
    return lax.all_to_all(
        jnp.broadcast_to(value[None], (4,) + value.shape), axis, 0, 0, tiled=True
    )


def left_source(core):
    def target(x, c, z, y):
        if x // 2 != z:
            return None
        there = 2 * (x % 2) + c
        return ((y - there) % 4, core, z, there)

    return pairs(("x", "core", "zh", "y"), target)


def shaped(shape, dtype):
    return jax.ShapeDtypeStruct(shape, dtype)


def call(
    kernel, outs, where, *operands, after=(), scratch=(), flops=0, moved=0, limit=16
):
    n = len(operands)

    def inner(*refs):
        kernel(*refs[: n + 1], *refs[n + 1 + len(after) :])

    return pl.pallas_call(
        inner,
        out_shape=outs,
        in_specs=[pl.BlockSpec(memory_space=pltpu.SMEM)]
        + [pl.BlockSpec(memory_space=pltpu.VMEM)] * n
        + [pl.BlockSpec(memory_space=pl.ANY)] * len(after),
        scratch_shapes=scratch,
        compiler_params=pltpu.CompilerParams(vmem_limit_bytes=limit * 1024 * 1024),
        cost_estimate=pl.CostEstimate(
            flops=flops, bytes_accessed=moved, transcendentals=0
        ),
    )(where, *operands, *after)


def first_kernel(where, grad, right, first, second, mine, moments):
    mine[:640] = grad[...]
    mine[640:] = right[pl.ds(pl.multiple_of(where[0] * 128, 128), 128)]
    moments[0] = first[...].astype(bf16)
    moments[1] = second[...].astype(bf16)


def left_kernel(where, near, far, grad, left, keep, send, slabs, panel):
    core, z = where[1], where[2]
    for k in range(4):
        slabs[:, 128 * k : 128 * k + 128] = near[k, 640:]
        slabs[:, 512 + 128 * k : 640 + 128 * k] = far[k, 640:]
        panel[:, 128 * k : 128 * k + 128] = near[k, :640]
        panel[:, 512 + 128 * k : 640 + 128 * k] = far[k, :640]

    product = dot(left[...], panel[...], 0, 0).astype(bf16)
    gram = (dot(grad[...], panel[...], 0, 0) * (1.0 / M)).astype(bf16)

    def columns(t, flip):
        found = []
        for k in range(4):
            block = 2 * k + t
            if flip:
                block = (block + 4) % 8
            at = block * 128
            found += [gram[:64, at : at + 128], gram[64:, at : at + 128]]
        return jnp.concatenate(found, axis=1)

    for c in range(2):

        @pl.when(core == c)
        def _():
            keep[:320] = product[320 * c : 320 * c + 320]
            send[:320] = product[320 * (1 - c) : 320 * (1 - c) + 320]
            for half in range(2):

                @pl.when(z == half)
                def _():
                    keep[320:] = columns(c, half == 1)
                    send[320:] = columns(1 - c, half == 1)


def join_kernel(where, first, second, four):
    for k in range(4):
        at = slice(256 * k, 256 * k + 256)
        four[k] = (first[:, at].astype(f32) + second[:, at].astype(f32)).astype(bf16)


def sum_kernel(where, parts, rows, gram):
    total = (
        parts[0].astype(f32)
        + parts[1].astype(f32)
        + parts[2].astype(f32)
        + parts[3].astype(f32)
    )
    mine = total[:320].astype(bf16)
    for k in range(4):
        rows[k] = mine
    gram[:64] = total[320:, :128]
    gram[64:] = total[320:, 128:]


def turn_kernel(where, half, moments, basis, out, own, rows, rotated):
    row, core = where[0], where[1]
    for k in range(4):
        rows[:, 256 * k : 256 * k + 256] = half[k]
    rotated[...] = dot(rows[...], basis[...], 1, 1)
    next_row = row + 1 - 2 * core
    own[...] = rotated[:, pl.ds(pl.multiple_of(row * 128, 128), 128)]
    theirs = rotated[:, pl.ds(pl.multiple_of(next_row * 128, 128), 128)]
    out[:, 1024:] = theirs.astype(bf16)
    for i in range(8):
        turned = rotated[:, 128 * i : 128 * i + 128]
        old, old_sq = moments[i, 0].astype(f32), moments[i, 1].astype(f32)
        new = first_beta * old + (1.0 - first_beta) * turned
        new_sq = second_beta * old_sq + (1.0 - second_beta) * turned * turned
        rows[:, 128 * i : 128 * i + 128] = (new / (jnp.sqrt(new_sq) + epsilon)).astype(bf16)
    out[:, :1024] = dot(rows[...], basis[...], 1, 0).astype(bf16)


def back_kernel(where, left, mine, other, out, joined):
    core = where[1]
    joined[pl.ds(pl.multiple_of(core * 320, 320), 320)] = mine[:, :1024]
    joined[pl.ds(pl.multiple_of(320 - core * 320, 320), 320)] = other[:, :1024]
    product = dot(left[...], joined[...], 1, 0).astype(bf16)
    for k in range(4):
        out[k, :640] = product[:, 128 * k : 128 * k + 128]
        out[k, 640:] = product[:, 512 + 128 * k : 640 + 128 * k]


def fold(parts, rows):
    return (
        parts[0, rows].astype(f32)
        + parts[1, rows].astype(f32)
        + parts[2, rows].astype(f32)
        + parts[3, rows].astype(f32)
    )


def fold_kernel(where, parts, send):
    send[...] = fold(parts, slice(640, 1280)).astype(bf16)


def moments_kernel(
    where, own, other, first, second, parts, first_new, second_new, kept
):
    core = where[1]
    kept[...] = fold(parts, slice(0, 640))
    theirs = other[:, 1024:].astype(f32)
    for value, at in ((own[...], core * 320), (theirs, 320 - core * 320)):
        rows = pl.ds(pl.multiple_of(at, 320), 320)
        first_new[rows] = first_beta * first[rows] + (1.0 - first_beta) * value
        second_new[rows] = (
            second_beta * second[rows] + (1.0 - second_beta) * value * value
        )


def pair_kernel(where, first, second, out, mark):
    out[...] = first[...] + second[...]
    mark[...] = jnp.zeros_like(mark)


def gram_kernel(where, near, far, paired, out, panel, other):
    for k in range(4):
        panel[:, 128 * k : 128 * k + 128] = near[k, :640]
        panel[:, 512 + 128 * k : 640 + 128 * k] = far[k, :640]
    for k in range(8):
        other[:, 128 * k : 128 * k + 128] = paired[k]
    out[...] = dot(panel[...], other[...], 1, 1) * (1.0 / C)


def body(grad, left_basis, right_rows, exp_avg, exp_avg_sq):
    x, core = lax.axis_index("x"), lax.axis_index("core")
    z, y = lax.axis_index("zh"), lax.axis_index("y")
    row = 2 * x + core
    where = jnp.stack([row, core, z, y]).astype(jnp.int32)

    mine, moments = call(
        first_kernel,
        [shaped((768, 128), bf16), shaped((2, 640, 128), bf16)],
        where,
        grad,
        right_rows,
        exp_avg,
        exp_avg_sq,
        moved=1_500_000,
        limit=60,
    )
    far = other_half(mine)
    near_all = lax.all_gather(mine, "y", axis=0)

    moments = lax.all_gather(moments, ROW, axis=0)
    far_all = lax.all_gather(far, "y", axis=0)

    keep, send, slabs = call(
        left_kernel,
        [shaped((384, 1024), bf16)] * 2 + [shaped((128, 1024), bf16)],
        where,
        near_all,
        far_all,
        grad,
        left_basis,
        scratch=[pltpu.VMEM((640, 1024), bf16)],
        flops=1_000_000_000,
        moved=5_000_000,
    )
    basis = lax.all_gather(slabs, ROW, axis=0, tiled=True)
    moments = lax.dynamic_slice_in_dim(moments, core * 320, 320, 2)
    (summed,) = call(
        join_kernel,
        [shaped((4, 384, 256), bf16)],
        where,
        keep,
        other_core(send),
        after=(moments,),
        moved=2_400_000,
    )
    summed = lax.all_to_all(summed, "x", 0, 0, tiled=True)

    axes = ("x", "core", "zh", "y")
    to_x = (y + 8 - 2 * (x % 2) - core) % 4
    at = 2 * (to_x % 2)

    def piece(t):
        return jnp.where(
            to_x < 2,
            lax.dynamic_index_in_dim(near_all, at + t, 0, False)[:640],
            lax.dynamic_index_in_dim(far_all, at + t, 0, False)[:640],
        )

    pair, paired_mark = call(
        pair_kernel,
        [shaped((640, 128), bf16), shaped((8, 128), f32)],
        where,
        *[lax.ppermute(piece(t), axes, left_source(t)) for t in range(2)],
        moved=500_000,
    )

    rows, right_gram = call(
        sum_kernel,
        [shaped((4, 320, 256), bf16), shaped((128, 128), f32)],
        where,
        summed,
        moved=1_500_000,
    )
    half = lax.all_to_all(rows, "x", 0, 0, tiled=True)

    turned, own = call(
        turn_kernel,
        [shaped((320, 1152), bf16), shaped((320, 128), f32)],
        where,
        half,
        moments,
        basis,
        after=(paired_mark,),
        scratch=[pltpu.VMEM((320, 1024), bf16), pltpu.VMEM((320, 1024), f32)],
        flops=1_400_000_000,
        moved=6_000_000,
    )
    turned_far = other_core(turned)
    (parts,) = call(
        back_kernel,
        [shaped((4, 1280, 128), bf16)],
        where,
        left_basis,
        turned,
        turned_far,
        scratch=[pltpu.VMEM((640, 1024), bf16)],
        flops=840_000_000,
        moved=4_000_000,
    )
    parts = lax.all_to_all(parts, "y", 0, 0, tiled=True)
    (send,) = call(
        fold_kernel, [shaped((640, 128), bf16)], where, parts, moved=1_400_000
    )
    arrived = other_half(send)

    paired = lax.all_gather(pair, ROW, axis=0)
    (left_gram,) = call(
        gram_kernel,
        [shaped((640, 640), f32)],
        where,
        near_all,
        far_all,
        paired,
        after=(send,),
        scratch=[pltpu.VMEM((640, 1024), bf16), pltpu.VMEM((640, 1024), bf16)],
        flops=10_000,
        moved=10_000,
    )
    exp_avg_new, exp_avg_sq_new, kept = call(
        moments_kernel,
        [shaped((640, 128), f32)] * 3,
        where,
        own,
        turned_far,
        exp_avg,
        exp_avg_sq,
        parts,
        moved=10_000,
    )

    update = (kept + arrived.astype(f32)).astype(bf16)
    return (update, exp_avg_new, exp_avg_sq_new, left_gram, right_gram)


def solution(mesh):
    wide = Mesh(
        mesh.devices.reshape(8, 4, 2, 2, 4), ("layer", "x", "core", "zh", "y")
    )
    row, col = ("x", "core"), ("zh", "y")
    return jax.shard_map(
        body,
        mesh=wide,
        in_specs=(
            P(("layer",) + row, col),
            P(("layer",) + row, col),
            P("layer", col),
            P(("layer",) + col, row),
            P(("layer",) + col, row),
        ),
        out_specs=(
            P(("layer",) + row, col),
            P(("layer",) + col, row),
            P(("layer",) + col, row),
            P(("layer",) + row, col),
            P(("layer",) + col, row),
        ),
        check_vma=False,
    )
```

```python
import itertools

import jax
import jax.numpy as jnp
from jax import lax
from jax.experimental import pallas as pl
from jax.experimental.pallas import tpu as pltpu
from jax.sharding import Mesh, PartitionSpec as P

M = 5120
C = 1024

first_beta = 0.9
second_beta = 0.95
epsilon = 1e-08

SIZES = {"x": 4, "core": 2, "zh": 2, "y": 4}
ROW = ("x", "core")
f32 = jnp.float32
bf16 = jnp.bfloat16


def pairs(axes, target):
    found = []
    for place in itertools.product(*[range(SIZES[a]) for a in axes]):
        there = target(*place)
        if there is None:
            continue
        src = dst = 0
        for a, s, d in zip(axes, place, there):
            src, dst = src * SIZES[a] + s, dst * SIZES[a] + d
        found.append((src, dst))
    return found


def dot(a, b, over_a, over_b):
    return lax.dot_general(
        a, b, (((over_a,), (over_b,)), ((), ())), preferred_element_type=f32
    )


def other_core(value):
    return lax.ppermute(value, "core", [(0, 1), (1, 0)])


def other_half(value):
    return lax.ppermute(value, "zh", [(0, 1), (1, 0)])


def spread(value, axis):
    return lax.all_to_all(
        jnp.broadcast_to(value[None], (4,) + value.shape), axis, 0, 0, tiled=True
    )


def left_source(core):
    def target(x, c, z, y):
        if x // 2 != z:
            return None
        there = 2 * (x % 2) + c
        return ((y - there) % 4, core, z, there)

    return pairs(("x", "core", "zh", "y"), target)


def shaped(shape, dtype):
    return jax.ShapeDtypeStruct(shape, dtype)


def call(
    kernel, outs, where, *operands, after=(), scratch=(), flops=0, moved=0, limit=16
):
    n = len(operands)

    def inner(*refs):
        kernel(*refs[: n + 1], *refs[n + 1 + len(after) :])

    return pl.pallas_call(
        inner,
        out_shape=outs,
        in_specs=[pl.BlockSpec(memory_space=pltpu.SMEM)]
        + [pl.BlockSpec(memory_space=pltpu.VMEM)] * n
        + [pl.BlockSpec(memory_space=pl.ANY)] * len(after),
        scratch_shapes=scratch,
        compiler_params=pltpu.CompilerParams(vmem_limit_bytes=limit * 1024 * 1024),
        cost_estimate=pl.CostEstimate(
            flops=flops, bytes_accessed=moved, transcendentals=0
        ),
    )(where, *operands, *after)


def first_kernel(where, grad, right, first, second, mine, moments):
    mine[:640] = grad[...]
    mine[640:] = right[pl.ds(pl.multiple_of(where[0] * 128, 128), 128)]
    moments[0] = first[...].astype(bf16)
    moments[1] = second[...].astype(bf16)


def left_kernel(where, near, far, grad, left, keep, send, slabs, panel):
    core, z = where[1], where[2]
    for k in range(4):
        slabs[:, 128 * k : 128 * k + 128] = near[k, 640:]
        slabs[:, 512 + 128 * k : 640 + 128 * k] = far[k, 640:]
        panel[:, 128 * k : 128 * k + 128] = near[k, :640]
        panel[:, 512 + 128 * k : 640 + 128 * k] = far[k, :640]

    product = dot(left[...], panel[...], 0, 0).astype(bf16)
    gram = (dot(grad[...], panel[...], 0, 0) * (1.0 / M)).astype(bf16)

    def columns(t, flip):
        found = []
        for k in range(4):
            block = 2 * k + t
            if flip:
                block = (block + 4) % 8
            at = block * 128
            found += [gram[:64, at : at + 128], gram[64:, at : at + 128]]
        return jnp.concatenate(found, axis=1)

    for c in range(2):

        @pl.when(core == c)
        def _():
            keep[:320] = product[320 * c : 320 * c + 320]
            send[:320] = product[320 * (1 - c) : 320 * (1 - c) + 320]
            for half in range(2):

                @pl.when(z == half)
                def _():
                    keep[320:] = columns(c, half == 1)
                    send[320:] = columns(1 - c, half == 1)


def join_kernel(where, first, second, four):
    for k in range(4):
        at = slice(256 * k, 256 * k + 256)
        four[k] = (first[:, at].astype(f32) + second[:, at].astype(f32)).astype(bf16)


def sum_kernel(where, parts, rows, gram):
    total = (
        parts[0].astype(f32)
        + parts[1].astype(f32)
        + parts[2].astype(f32)
        + parts[3].astype(f32)
    )
    mine = total[:320].astype(bf16)
    for k in range(4):
        rows[k] = mine
    gram[:64] = total[320:, :128]
    gram[64:] = total[320:, 128:]


def turn_kernel(where, half, moments, basis, out, own, rows, rotated):
    row, core = where[0], where[1]
    for k in range(4):
        rows[:, 256 * k : 256 * k + 256] = half[k]
    rotated[...] = dot(rows[...], basis[...], 1, 1)
    next_row = row + 1 - 2 * core
    own[...] = rotated[:, pl.ds(pl.multiple_of(row * 128, 128), 128)]
    theirs = rotated[:, pl.ds(pl.multiple_of(next_row * 128, 128), 128)]
    out[:, 1024:] = theirs.astype(bf16)
    for i in range(8):
        turned = rotated[:, 128 * i : 128 * i + 128]
        old, old_sq = moments[i, 0].astype(f32), moments[i, 1].astype(f32)
        new = first_beta * old + (1.0 - first_beta) * turned
        new_sq = second_beta * old_sq + (1.0 - second_beta) * turned * turned
        rows[:, 128 * i : 128 * i + 128] = (new / (jnp.sqrt(new_sq) + epsilon)).astype(bf16)
    out[:, :1024] = dot(rows[...], basis[...], 1, 0).astype(bf16)


def back_kernel(where, left, mine, other, out, joined):
    core = where[1]
    joined[pl.ds(pl.multiple_of(core * 320, 320), 320)] = mine[:, :1024]
    joined[pl.ds(pl.multiple_of(320 - core * 320, 320), 320)] = other[:, :1024]
    product = dot(left[...], joined[...], 1, 0).astype(bf16)
    for k in range(4):
        out[k, :640] = product[:, 128 * k : 128 * k + 128]
        out[k, 640:] = product[:, 512 + 128 * k : 640 + 128 * k]


def fold(parts, rows):
    return (
        parts[0, rows].astype(f32)
        + parts[1, rows].astype(f32)
        + parts[2, rows].astype(f32)
        + parts[3, rows].astype(f32)
    )


def fold_kernel(where, parts, send):
    send[...] = fold(parts, slice(640, 1280)).astype(bf16)


def moments_kernel(
    where, own, other, first, second, parts, first_new, second_new, kept
):
    core = where[1]
    kept[...] = fold(parts, slice(0, 640))
    theirs = other[:, 1024:].astype(f32)
    for value, at in ((own[...], core * 320), (theirs, 320 - core * 320)):
        rows = pl.ds(pl.multiple_of(at, 320), 320)
        first_new[rows] = first_beta * first[rows] + (1.0 - first_beta) * value
        second_new[rows] = (
            second_beta * second[rows] + (1.0 - second_beta) * value * value
        )


def gram_kernel(where, near, far, paired, out, panel, other):
    for k in range(4):
        panel[:, 128 * k : 128 * k + 128] = near[k, :640]
        panel[:, 512 + 128 * k : 640 + 128 * k] = far[k, :640]
    for k in range(8):
        other[:, 128 * k : 128 * k + 128] = paired[k]
    out[...] = dot(panel[...], other[...], 1, 1) * (1.0 / C)


def body(grad, left_basis, right_rows, exp_avg, exp_avg_sq):
    x, core = lax.axis_index("x"), lax.axis_index("core")
    z, y = lax.axis_index("zh"), lax.axis_index("y")
    row = 2 * x + core
    where = jnp.stack([row, core, z, y]).astype(jnp.int32)

    mine, moments = call(
        first_kernel,
        [shaped((768, 128), bf16), shaped((2, 640, 128), bf16)],
        where,
        grad,
        right_rows,
        exp_avg,
        exp_avg_sq,
        moved=1_500_000,
        limit=60,
    )
    far = other_half(mine)
    near_all = lax.all_gather(mine, "y", axis=0)

    moments = lax.all_gather(moments, ROW, axis=0)
    far_all = lax.all_gather(far, "y", axis=0)

    keep, send, slabs = call(
        left_kernel,
        [shaped((384, 1024), bf16)] * 2 + [shaped((128, 1024), bf16)],
        where,
        near_all,
        far_all,
        grad,
        left_basis,
        scratch=[pltpu.VMEM((640, 1024), bf16)],
        flops=1_000_000_000,
        moved=5_000_000,
    )
    basis = lax.all_gather(slabs, ROW, axis=0, tiled=True)
    moments = lax.dynamic_slice_in_dim(moments, core * 320, 320, 2)
    (summed,) = call(
        join_kernel,
        [shaped((4, 384, 256), bf16)],
        where,
        keep,
        other_core(send),
        after=(moments,),
        moved=2_400_000,
    )
    summed = lax.all_to_all(summed, "x", 0, 0, tiled=True)

    axes = ("x", "core", "zh", "y")
    to_x = (y + 8 - 2 * (x % 2) - core) % 4
    at = 2 * (to_x % 2)

    def piece(t):
        return jnp.where(
            to_x < 2,
            lax.dynamic_index_in_dim(near_all, at + t, 0, False)[:640],
            lax.dynamic_index_in_dim(far_all, at + t, 0, False)[:640],
        )

    pair = lax.ppermute(piece(0), axes, left_source(0)) + lax.ppermute(
        piece(1), axes, left_source(1)
    )

    rows, right_gram = call(
        sum_kernel,
        [shaped((4, 320, 256), bf16), shaped((128, 128), f32)],
        where,
        summed,
        moved=1_500_000,
    )
    half = lax.all_to_all(rows, "x", 0, 0, tiled=True)

    turned, own = call(
        turn_kernel,
        [shaped((320, 1152), bf16), shaped((320, 128), f32)],
        where,
        half,
        moments,
        basis,
        after=(pair[:16],),
        scratch=[pltpu.VMEM((320, 1024), bf16), pltpu.VMEM((320, 1024), f32)],
        flops=1_400_000_000,
        moved=6_000_000,
    )
    turned_far = other_core(turned)
    (parts,) = call(
        back_kernel,
        [shaped((4, 1280, 128), bf16)],
        where,
        left_basis,
        turned,
        turned_far,
        scratch=[pltpu.VMEM((640, 1024), bf16)],
        flops=840_000_000,
        moved=4_000_000,
    )
    parts = lax.all_to_all(parts, "y", 0, 0, tiled=True)
    (send,) = call(
        fold_kernel, [shaped((640, 128), bf16)], where, parts, moved=1_400_000
    )
    arrived = other_half(send)

    paired = lax.all_gather(pair, ROW, axis=0)
    (left_gram,) = call(
        gram_kernel,
        [shaped((640, 640), f32)],
        where,
        near_all,
        far_all,
        paired,
        after=(send,),
        scratch=[pltpu.VMEM((640, 1024), bf16), pltpu.VMEM((640, 1024), bf16)],
        flops=10_000,
        moved=10_000,
    )
    exp_avg_new, exp_avg_sq_new, kept = call(
        moments_kernel,
        [shaped((640, 128), f32)] * 3,
        where,
        own,
        turned_far,
        exp_avg,
        exp_avg_sq,
        parts,
        moved=10_000,
    )

    update = (kept + arrived.astype(f32)).astype(bf16)
    return (update, exp_avg_new, exp_avg_sq_new, left_gram, right_gram)


def solution(mesh):
    wide = Mesh(
        mesh.devices.reshape(8, 4, 2, 2, 4), ("layer", "x", "core", "zh", "y")
    )
    row, col = ("x", "core"), ("zh", "y")
    return jax.shard_map(
        body,
        mesh=wide,
        in_specs=(
            P(("layer",) + row, col),
            P(("layer",) + row, col),
            P("layer", col),
            P(("layer",) + col, row),
            P(("layer",) + col, row),
        ),
        out_specs=(
            P(("layer",) + row, col),
            P(("layer",) + col, row),
            P(("layer",) + col, row),
            P(("layer",) + row, col),
            P(("layer",) + col, row),
        ),
        check_vma=False,
    )
```
